128 devices in a mesh: row: 8 (over x_hi, y), col: 16 (over z, x_lo, core).
Axes of the slice: x: 4 (x_hi: 2, x_lo: 2; x = x_hi * 2 + x_lo), y: 4, z: 4, core: 2. Of those that a mesh axis runs over, the one named last changes fastest.
Arguments:
- pair: bfloat16 [640, 640, 128], P('row', 'col'), may hold values from -6 to 6
- block_chain: int32 [10], replicated, may hold values from 0 to 4, never falling along the last dimension, each value on 1 to 4 neighbouring positions
- block_valid: int32 [10], replicated, may hold values 0 or 1
- tri_norm_gain: float32 [128], replicated, may hold values from 0.25 to 1.75
- tri_norm_bias: float32 [128], replicated, may hold values from -3 to 3
- tri_in_weight: bfloat16 [128, 512], replicated, may hold values from -0.5 to 0.5
- tri_gate_weight: bfloat16 [128, 128], replicated, may hold values from -0.5 to 0.5
- out_norm_gain: float32 [128], replicated, may hold values from 0.25 to 1.75
- out_norm_bias: float32 [128], replicated, may hold values from -3 to 3
- tri_out_weight: bfloat16 [128, 128], replicated, may hold values from -0.5 to 0.5
- att_norm_gain: float32 [128], replicated, may hold values from 0.25 to 1.75
- att_norm_bias: float32 [128], replicated, may hold values from -3 to 3
- qkvg_weight: bfloat16 [128, 512], replicated, may hold values from -0.5 to 0.5
- bias_weight: bfloat16 [128, 4], replicated, may hold values from -1 to 1
- inter_chain: float32 [4], replicated, may hold values from -3 to 3
- att_out_weight: bfloat16 [128, 128], replicated, may hold values from -0.5 to 0.5
Outputs:
- pair_out: bfloat16 [640, 640, 128], P('row', 'col')
The draws below stay inside these ranges and needn't reach their ends.
Inputs may be any that keep to these rules, and one draw needn't show every extreme that they name: `block_chain`: chain numbers never fall along the crop; each chain covers 1 to 4 blocks and every number from 0 up appears.
All inputs are finite; a program needn't handle non-finite values.
Results may differ from the reference program's by a relative error of at most 0.0095.
Values may be sent and summed in bfloat16 or wider, within the bound.
No kernel may reach another device: no remote copies, remote signals or barrier semaphores. Data moves between devices by JAX's collectives and lax.ppermute only.
A program may use at most 128 MiB of HBM per device.

```python
import math
import jax
import jax.numpy as jnp
import numpy as np
from jax import lax

C = 128
CH = 128
H = 4
DH = 32
MB = 64
N = 640
NBLK = 10
HD = 128


def with_ends(values, own_key, least, high):
    longest = values.shape.index(max(values.shape))
    spots = []
    for shift in (0, 1):
        where = [jax.random.randint(jax.random.fold_in(own_key, axis), (), 0, length) for axis, length in enumerate(values.shape)]
        where[longest] = (where[longest] + shift) % values.shape[longest]
        spots.append(tuple(where))
    return values.at[spots[0]].set(least).at[spots[1]].set(high)


def block_scale(rng, extent, pieces, smallest, top_value):
    factor_of = 1.0
    for axis_at, blocks in pieces:
        heights = jax.random.uniform(jax.random.fold_in(jax.random.fold_in(rng, 6), axis_at), (blocks,), jnp.float32, smallest / len(pieces), top_value / len(pieces))
        factor_of = factor_of * jnp.repeat(jnp.exp(heights), extent[axis_at] // blocks).reshape((-1,) + (1,) * (len(extent) - 1 - axis_at))
    return factor_of


def length_profile(number_of, total, most, skew):
    weights = [(1 << 20) // math.isqrt(grade ** skew) + 1 for grade in range(2, number_of + 1)]
    spare, given = total - most - (number_of - 1), [1] * (number_of - 1)
    while spare > 0:
        free = [i for i in range(number_of - 1) if given[i] < most]
        pool, left = sum([weights[i] for i in free]), spare
        for i in free:
            more = min(most - given[i], max(1, left * weights[i] // pool), spare)
            given[i] = given[i] + more
            spare = spare - more
    return np.array([most] + given)


def ragged(rng, amount, total, bound, skew):
    if amount == 2:
        one = jax.random.randint(rng, (), max(1, total - bound), min(bound, total - 1) + 1)
        return jnp.stack([one, total - one])
    sizes = jnp.asarray(length_profile(amount, total, bound, skew), jnp.int32)
    twos = (amount - 1) // 2
    donor, sink = sizes[1:1 + 2 * twos:2], sizes[2:2 + 2 * twos:2]
    room = jnp.minimum(donor - 1, bound - sink)
    moved = jax.random.randint(jax.random.fold_in(rng, 1), (twos,), 0, 1 << 20) % (room + 1)
    sizes = sizes.at[1:1 + 2 * twos:2].set(donor - moved).at[2:2 + 2 * twos:2].set(sink + moved)
    return sizes[jax.random.permutation(jax.random.fold_in(rng, 2), amount)]


def bell_draw(stream_key, extent, width, most, shards=(), kind=jnp.bfloat16):
    entries = jax.random.normal(stream_key, extent, jnp.float32) * width
    if len(shards) > 0:
        entries = block_scale(stream_key, extent, shards, -0.22, 0.18) * entries
    return jnp.clip(entries, min=-most, max=most).astype(kind)


def setup_inputs(seed: int = 0) -> dict:
    arg_keys = jax.random.split(jax.random.key(seed), 17)
    pair = bell_draw(arg_keys[0], (N, N, C), 1.0, 6.0, ((0, 8), (1, 16)))
    block_chain = jnp.searchsorted(jnp.cumsum(ragged(arg_keys[1], NBLK // 2, NBLK, 4, 0)), jnp.arange(NBLK), side="right").astype(jnp.int32)
    block_valid = with_ends((jax.random.randint(arg_keys[2], (NBLK,), 0, 4) < 3).astype(jnp.int32), jax.random.fold_in(arg_keys[2], 1), 0, 1)
    tri_norm_gain = jnp.clip(1.0 + 0.15 * jax.random.normal(arg_keys[3], (C,), jnp.float32), 0.25, 1.75)
    tri_norm_bias = bell_draw(arg_keys[4], (C,), 0.5, 3.0, (), jnp.float32)
    tri_in_weight = bell_draw(arg_keys[5], (C, 4 * CH), C ** -0.5, 0.5)
    tri_gate_weight = bell_draw(arg_keys[6], (C, C), C ** -0.5, 0.5)
    out_norm_gain = jnp.clip(1.0 + 0.15 * jax.random.normal(arg_keys[7], (CH,), jnp.float32), 0.25, 1.75)
    out_norm_bias = bell_draw(arg_keys[8], (CH,), 0.5, 3.0, (), jnp.float32)
    tri_out_weight = bell_draw(arg_keys[9], (CH, C), CH ** -0.5, 0.5)
    att_norm_gain = jnp.clip(1.0 + 0.15 * jax.random.normal(arg_keys[10], (C,), jnp.float32), 0.25, 1.75)
    att_norm_bias = bell_draw(arg_keys[11], (C,), 0.5, 3.0, (), jnp.float32)
    qkvg_weight = bell_draw(arg_keys[12], (C, 4 * HD), C ** -0.5, 0.5)
    bias_weight = bell_draw(arg_keys[13], (C, H), (C // 4) ** -0.5, 1.0)
    inter_chain = jnp.clip(jax.random.uniform(arg_keys[14], (H,), jnp.float32, -3.0, 3.0), -3.0, 3.0)
    att_out_weight = bell_draw(arg_keys[15], (HD, C), HD ** -0.5, 0.5)
    return {"pair": pair, "block_chain": block_chain, "block_valid": block_valid, "tri_norm_gain": tri_norm_gain, "tri_norm_bias": tri_norm_bias, "tri_in_weight": tri_in_weight, "tri_gate_weight": tri_gate_weight, "out_norm_gain": out_norm_gain, "out_norm_bias": out_norm_bias, "tri_out_weight": tri_out_weight, "att_norm_gain": att_norm_gain, "att_norm_bias": att_norm_bias, "qkvg_weight": qkvg_weight, "bias_weight": bias_weight, "inter_chain": inter_chain, "att_out_weight": att_out_weight}


MASK_NEG = 10000.0
EPS = 1e-05

def layer_norm(values, gain, shift):
    middle = lax.optimization_barrier(jnp.mean(values, axis=-1, keepdims=True))
    centred = values - middle
    spread = lax.optimization_barrier(jnp.mean(centred * centred, axis=-1, keepdims=True))
    return centred * lax.rsqrt(spread + EPS) * gain + shift

def extra_terms(bias_part, inter_chain, key_chain, query_chain, key_valid):
    crossing = (key_chain[:, None] != query_chain[None, :]).astype(jnp.float32)
    masking = MASK_NEG * (key_valid - 1.0)
    return bias_part.astype(jnp.float32) + inter_chain[:, None, None] * crossing[None] + masking[None, :, None]

def attend(queries, keys, values, extra):
    scores = jnp.einsum('khd,ihd->hki', keys.astype(jnp.float32), queries.astype(jnp.float32)) + extra
    highest = lax.optimization_barrier(jnp.max(scores, axis=1, keepdims=True))
    powers = jnp.exp(scores - highest)
    weights = (powers / lax.optimization_barrier(jnp.sum(powers, axis=1, keepdims=True))).astype(jnp.bfloat16)
    return jnp.einsum('hki,khd->ihd', weights.astype(jnp.float32), values.astype(jnp.float32))

def reference(pair, block_chain, block_valid, tri_norm_gain, tri_norm_bias, tri_in_weight, tri_gate_weight, out_norm_gain, out_norm_bias, tri_out_weight, att_norm_gain, att_norm_bias, qkvg_weight, bias_weight, inter_chain, att_out_weight):
    residue_valid = jnp.repeat(block_valid, MB).astype(jnp.float32)
    residue_chain = jnp.repeat(block_chain, MB)
    pair_mask = (residue_valid[:, None] * residue_valid[None, :])[:, :, None]
    tri_normed = layer_norm(pair.astype(jnp.float32), tri_norm_gain, tri_norm_bias).astype(jnp.bfloat16)
    flat_normed = tri_normed.reshape(N * N, C)
    tri_proj = jnp.dot(flat_normed, tri_in_weight, preferred_element_type=jnp.float32).reshape(N, N, 4 * CH)
    left_side = (pair_mask * jax.nn.sigmoid(tri_proj[:, :, :CH]) * tri_proj[:, :, CH:2 * CH]).astype(jnp.bfloat16)
    right_side = (pair_mask * jax.nn.sigmoid(tri_proj[:, :, 2 * CH:3 * CH]) * tri_proj[:, :, 3 * CH:]).astype(jnp.bfloat16)
    tri_gate = jax.nn.sigmoid(jnp.dot(flat_normed, tri_gate_weight, preferred_element_type=jnp.float32)).reshape(N, N, C)
    product = jnp.einsum('ikc,jkc->ijc', left_side.astype(jnp.float32), right_side.astype(jnp.float32))
    product_normed = layer_norm(product, out_norm_gain, out_norm_bias).astype(jnp.bfloat16)
    update = jnp.dot(product_normed.reshape(N * N, CH), tri_out_weight, preferred_element_type=jnp.float32).reshape(N, N, C)
    pair_mid = (pair.astype(jnp.float32) + tri_gate * update).astype(jnp.bfloat16)
    att_normed = layer_norm(pair_mid.astype(jnp.float32), att_norm_gain, att_norm_bias).astype(jnp.bfloat16)
    flat_att = att_normed.reshape(N * N, C)
    projected = jnp.dot(flat_att, qkvg_weight, preferred_element_type=jnp.float32).reshape(N, N, 4, H, DH)
    queries = (projected[:, :, 0] * DH ** (-0.5)).astype(jnp.bfloat16)
    keys = projected[:, :, 1].astype(jnp.bfloat16)
    values = projected[:, :, 2].astype(jnp.bfloat16)
    gate_values = jax.nn.sigmoid(projected[:, :, 3]).reshape(N, N, HD)
    pair_bias = jnp.dot(flat_att, bias_weight, preferred_element_type=jnp.float32).astype(jnp.bfloat16).reshape(N, N, H)
    extra_full = extra_terms(jnp.transpose(pair_bias, (2, 0, 1)), inter_chain, residue_chain, residue_chain, residue_valid)

    def one_column(parts):
        return attend(parts[0], parts[1], parts[2], extra_full)
    results = lax.map(one_column, (jnp.swapaxes(queries, 0, 1), jnp.swapaxes(keys, 0, 1), jnp.swapaxes(values, 0, 1)))
    attended = jnp.swapaxes(results.reshape(N, N, HD), 0, 1)
    gated = (gate_values * attended).astype(jnp.bfloat16)
    final_update = jnp.dot(gated.reshape(N * N, HD), att_out_weight, preferred_element_type=jnp.float32).reshape(N, N, C)
    return (pair_mid.astype(jnp.float32) + pair_mask * final_update).astype(jnp.bfloat16)
```

```python
import functools

import jax
import jax.numpy as jnp
from jax import lax
from jax.experimental import pallas as pl
from jax.experimental.pallas import tpu as pltpu
from jax.sharding import PartitionSpec as P

H = 4
DH = 32
MB = 64
C = 128
N = 640
ROWS = 8
COLS = 16
RI = N // ROWS
CJ = N // COLS
T = CJ // ROWS
L = N // C
SEND = 56
BACK = 32
PAY = 24
CHUNK = RI

MASK_NEG = 10000.0
EPS = 1e-05

F32 = jnp.float32
BF16 = jnp.bfloat16
PARAMS = pltpu.CompilerParams(vmem_limit_bytes=48 * 1024 * 1024)
VMEM = pl.BlockSpec(memory_space=pltpu.VMEM)
SMEM = pl.BlockSpec(memory_space=pltpu.SMEM)


def dot(a, b, over):
    return lax.dot_general(a, b, (over, ((), ())), preferred_element_type=F32)


def layer_norm(values, gain, shift, axis=-1):
    middle = jnp.mean(values, axis=axis, keepdims=True)
    centred = values - middle
    spread = jnp.mean(centred * centred, axis=axis, keepdims=True)
    return centred * lax.rsqrt(spread + EPS) * gain + shift


def sigmoid(x):
    return 0.5 * jnp.tanh(0.5 * x) + 0.5


def call(kernel, out_shape, scratch, specs, cost=None):
    return pl.pallas_call(
        kernel,
        out_shape=out_shape,
        in_specs=specs,
        out_specs=jax.tree.map(lambda _: VMEM, out_shape),
        scratch_shapes=scratch,
        compiler_params=PARAMS,
        cost_estimate=cost,
    )


def struct(shape, dtype=BF16):
    return jax.ShapeDtypeStruct(shape, dtype)


def turn_kernel(pair_ref, out_ref, wide):
    wide[...] = pair_ref[...].astype(F32).reshape(RI * CJ, C)
    for j in range(CJ):
        out_ref[j] = wide[pl.ds(j, RI, stride=CJ), :].astype(BF16)


def turn_back_kernel(in_ref, out_ref, wide):
    for j in range(CJ):
        wide[pl.ds(j, RI, stride=CJ), :] = in_ref[j].astype(F32)
    out_ref[...] = wide[...].reshape(RI, CJ, C).astype(BF16)


def column(ref, t):
    return jnp.concatenate([ref[r * T + t] for r in range(ROWS)], axis=0)


def project_kernel(x_ref, valid_t_ref, valid_ref, gain_ref, bias_ref, w_ref, out_ref, wide):
    wide[...] = jnp.zeros_like(wide)
    for t in range(T):
        x = column(x_ref, t).astype(F32)
        normed = layer_norm(x, gain_ref[...], bias_ref[...]).astype(BF16)
        proj = dot(w_ref[...], normed, ((1,), (1,)))
        mask = valid_ref[...] * valid_t_ref[t]
        for side in range(2):
            gate = proj[2 * side * C : (2 * side + 1) * C]
            value = proj[(2 * side + 1) * C : (2 * side + 2) * C]
            part = mask * sigmoid(gate) * value
            for l in range(L):
                wide[pl.ds(side * T * L + t * L + l, C, stride=SEND), :] = part[
                    :, l * C : (l + 1) * C
                ]
    out_ref[...] = wide[...].reshape(C, SEND, C).astype(BF16)


def gate_kernel(x_ref, gain_ref, bias_ref, w_ref, out_ref):
    for t in range(T):
        x = column(x_ref, t).astype(F32)
        normed = layer_norm(x, gain_ref[...], bias_ref[...]).astype(BF16)
        out_ref[t] = sigmoid(dot(normed, w_ref[...], ((1,), (0,))))


def product_kernel(in_ref, out_ref, wide, left, right, prod, back):
    wide[...] = in_ref[...].astype(F32).reshape(C * SEND, C)
    for t in range(T):
        for l in range(L):
            left[t * C : (t + 1) * C, l * C : (l + 1) * C] = wide[
                pl.ds(t * L + l, C, stride=SEND), :
            ].astype(BF16)
            right[t * C : (t + 1) * C, l * C : (l + 1) * C] = wide[
                pl.ds(T * L + t * L + l, C, stride=SEND), :
            ].astype(BF16)
    back[...] = jnp.zeros_like(back)
    for l in range(L):
        prod[l] = dot(right[...], left[:, l * C : (l + 1) * C], ((0,), (0,)))
        for t in range(T):
            back[pl.ds(t * L + l, C, stride=BACK), :] = prod[l, pl.ds(t, C, stride=T), :]
    out_ref[...] = back[...].reshape(C, BACK, C).astype(BF16)


def middle_kernel(
    in_ref, x_ref, gate_ref, gain_ref, bias_ref, w_ref, gain2_ref, bias2_ref, wb_ref,
    mid_ref, att_ref, pay_ref, wide,
):
    wide[...] = in_ref[...].astype(F32).reshape(C * BACK, C)
    for t in range(T):
        prod = jnp.concatenate(
            [wide[pl.ds(t * L + l, C, stride=BACK), :] for l in range(L)], axis=1
        )
        normed = layer_norm(prod, gain_ref[...], bias_ref[...], 0).astype(BF16)
        update = dot(normed, w_ref[...], ((0,), (0,)))
        mid = (column(x_ref, t).astype(F32) + gate_ref[t] * update).astype(BF16)
        att = layer_norm(mid.astype(F32), gain2_ref[...], bias2_ref[...]).astype(BF16)
        mid_ref[t] = mid
        att_ref[t] = att
        rows = dot(wb_ref[...], att, ((1,), (1,)))
        for h in range(H):
            pay_ref[h * T + t : h * T + t + 1, :] = rows[h : h + 1].astype(BF16)
    pay_ref[H * T : PAY, :] = jnp.zeros((PAY - H * T, N), BF16)


def qkvg_kernel(att_ref, wqvg_ref, wk_ref, q_ref, k_ref, v_ref, g_ref):
    for t in range(T):
        att = att_ref[t]
        qvg = dot(att, wqvg_ref[...], ((1,), (0,)))
        q_ref[t] = (qvg[:, :C] * DH ** (-0.5)).astype(BF16)
        v_ref[t] = jnp.concatenate(
            [qvg[:, C : 2 * C].astype(BF16), jnp.ones((N, C), BF16)], axis=1
        )
        g_ref[t] = sigmoid(qvg[:, 2 * C :])
        k_ref[t] = dot(wk_ref[...], att, ((1,), (1,))).astype(BF16)


def merge_kernel(me_ref, spread_ref, *refs):
    parts, out_ref, all_rows = refs[:ROWS], refs[ROWS], refs[ROWS + 1]
    for d in range(ROWS):
        all_rows[me_ref[0] ^ d] = parts[d][...].astype(F32)
    rows = all_rows[...].reshape(ROWS * PAY, N).astype(BF16)
    out_ref[...] = dot(spread_ref[...], rows, ((1,), (0,))).astype(BF16)


def attend_kernel(
    me_ref, inter_ref, q_ref, k_ref, v_ref, g_ref, mid_ref, cross_ref, key_ref, valid_ref, valid_t_ref, wo_ref,
    *refs,
):
    parts, out_ref, extra = refs[:COLS], refs[COLS], refs[COLS + 1]
    for d in range(COLS):
        first = (me_ref[0] ^ d) * CJ
        for h in range(H):
            for s in range(CJ // 8):
                at = pl.multiple_of(first + 8 * s, 8)
                crossing = cross_ref[pl.ds(at // MB, 1), :]
                extra[h, pl.ds(at, 8), :] = (
                    parts[d][h * CJ + 8 * s : h * CJ + 8 * s + 8, :].astype(F32)
                    + inter_ref[h] * crossing
                    + key_ref[...]
                )
    lane_head = lax.broadcasted_iota(jnp.int32, (CHUNK, C), 1) // DH

    def one_column(t, carry):
        keys, vals = k_ref[t], v_ref[t]
        for n in range(N // CHUNK):
            rows = slice(n * CHUNK, (n + 1) * CHUNK)
            queries = q_ref[t, rows, :]
            total = jnp.zeros((CHUNK, C), F32)
            for h in range(H):
                own = jnp.where(lane_head == h, queries, jnp.zeros_like(queries))
                scores = dot(own, keys, ((1,), (0,))) + extra[h, rows, :]
                powers = jnp.exp(scores - jnp.max(scores, axis=1, keepdims=True)).astype(BF16)
                sums = dot(powers, vals, ((1,), (0,)))
                total = jnp.where(lane_head == h, sums[:, :C] / sums[:, C:], total)
            gated = (g_ref[t, rows, :] * total).astype(BF16)
            update = dot(gated, wo_ref[...], ((1,), (0,)))
            mask = valid_ref[rows, :] * valid_t_ref[t]
            out_ref[n * T + t] = (mid_ref[t, rows, :].astype(F32) + mask * update).astype(BF16)
        return carry

    lax.fori_loop(0, T, one_column, 0)


def on_device(
    pair,
    block_chain,
    block_valid,
    tri_norm_gain,
    tri_norm_bias,
    tri_in_weight,
    tri_gate_weight,
    out_norm_gain,
    out_norm_bias,
    tri_out_weight,
    att_norm_gain,
    att_norm_bias,
    qkvg_weight,
    bias_weight,
    inter_chain,
    att_out_weight,
):
    row_at, col_at = lax.axis_index("row"), lax.axis_index("col")
    residue_valid = jnp.repeat(block_valid, MB).astype(F32)
    residue_chain = jnp.repeat(block_chain, MB)
    valid_t = lax.dynamic_slice_in_dim(residue_valid, (col_at * ROWS + row_at) * T, T)
    valid_lanes = residue_valid[None, :]
    valid_rows = jnp.broadcast_to(residue_valid[:, None], (N, C))
    cross = (block_chain[:, None] != residue_chain[None, :]).astype(F32)
    key_mask = (MASK_NEG * (residue_valid - 1.0))[None, :]
    gain1, bias1 = tri_norm_gain[None, :], tri_norm_bias[None, :]

    turned = call(turn_kernel, struct((CJ, RI, C)), [pltpu.VMEM((RI * CJ, C), F32)], [VMEM])(pair)
    x = lax.all_to_all(turned, "row", 0, 0, tiled=True)

    parcels = call(
        project_kernel,
        struct((C, SEND, C)),
        [pltpu.VMEM((C * SEND, C), F32)],
        [VMEM, SMEM, VMEM, VMEM, VMEM, VMEM],
    )(x, valid_t, valid_lanes, gain1, bias1, tri_in_weight.T)
    gate = call(gate_kernel, struct((T, N, C), F32), [], [VMEM] * 4)(
        x, gain1, bias1, tri_gate_weight
    )
    channel = lax.all_to_all(parcels, ("col", "row"), 0, 0, tiled=True)
    product = call(
        product_kernel,
        struct((C, BACK, C)),
        [
            pltpu.VMEM((C * SEND, C), F32),
            pltpu.VMEM((N, N), BF16),
            pltpu.VMEM((N, N), BF16),
            pltpu.VMEM((L, N, C), F32),
            pltpu.VMEM((C * BACK, C), F32),
        ],
        [VMEM],
    )(channel)
    returned = lax.all_to_all(product, ("col", "row"), 0, 0, tiled=True)

    wb = jnp.zeros((8, C), BF16).at[:H].set(bias_weight.T)
    mid, att, pay = call(
        middle_kernel,
        [struct((T, N, C)), struct((T, N, C)), struct((PAY, N))],
        [pltpu.VMEM((C * BACK, C), F32)],
        [VMEM] * 9,
    )(
        returned, x, gate, out_norm_gain[:, None], out_norm_bias[:, None], tri_out_weight,
        att_norm_gain[None, :], att_norm_bias[None, :], wb,
    )

    both = ("row", "col")

    def swap(values, row_xor, col_xor):
        pairs = [
            (r * COLS + c, (r ^ row_xor) * COLS + (c ^ col_xor))
            for r in range(ROWS)
            for c in range(COLS)
        ]
        return lax.ppermute(values, both, pairs)

    pays = [pay] + [swap(pay, d, 0) for d in range(1, ROWS)]
    wanted = jnp.arange(H * CJ)
    head, part, t = wanted // CJ, wanted % CJ // T, wanted % T
    spread = (
        (part * PAY + head * T + t)[:, None] == jnp.arange(ROWS * PAY)[None, :]
    ).astype(BF16)
    merged = call(
        merge_kernel,
        struct((H * CJ, N)),
        [pltpu.VMEM((ROWS, PAY, N), F32)],
        [SMEM] + [VMEM] * (ROWS + 1),
    )(row_at[None], spread, *pays)
    even = [merged] + [swap(merged, 0, d) for d in range(2, COLS, 2)]
    odd = [swap(one, 0, 1) for one in even]
    biases = [one for two in zip(even, odd) for one in two]

    wqvg = jnp.concatenate([qkvg_weight[:, :C], qkvg_weight[:, 2 * C :]], axis=1)
    q, k, v, g = call(
        qkvg_kernel,
        [struct((T, N, C)), struct((T, C, N)), struct((T, N, 2 * C)), struct((T, N, C), F32)],
        [],
        [VMEM] * 3,
    )(att, wqvg, qkvg_weight[:, C : 2 * C].T)

    out = call(
        attend_kernel,
        struct((CJ, RI, C)),
        [pltpu.VMEM((H, N, N), F32)],
        [SMEM, SMEM] + [VMEM] * 8 + [SMEM, VMEM] + [VMEM] * COLS,
    )(
        col_at[None], inter_chain, q, k, v, g, mid, cross, key_mask, valid_rows, valid_t, att_out_weight,
        *biases,
    )
    home = lax.all_to_all(out, "row", 0, 0, tiled=True)
    return call(turn_back_kernel, struct((RI, CJ, C)), [pltpu.VMEM((RI * CJ, C), F32)], [VMEM])(home)


def solution(mesh):
    placed = (P("row", "col", None),) + (P(),) * 15
    return jax.shard_map(
        on_device, mesh=mesh, in_specs=placed, out_specs=P("row", "col", None), check_vma=False
    )
```

```python
import functools

import jax
import jax.numpy as jnp
from jax import lax
from jax.experimental import pallas as pl
from jax.experimental.pallas import tpu as pltpu
from jax.sharding import PartitionSpec as P

H = 4
DH = 32
MB = 64
C = 128
N = 640
ROWS = 8
COLS = 16
RI = N // ROWS
CJ = N // COLS
T = CJ // ROWS
L = N // C
SEND = 56
BACK = 32
PAY = 24
GROUP = 4
CHUNK = GROUP * RI

MASK_NEG = 10000.0
EPS = 1e-05

F32 = jnp.float32
BF16 = jnp.bfloat16
VMEM = pl.BlockSpec(memory_space=pltpu.VMEM)
SMEM = pl.BlockSpec(memory_space=pltpu.SMEM)


def dot(a, b, over):
    return lax.dot_general(a, b, (over, ((), ())), preferred_element_type=F32)


def layer_norm(values, gain, shift, axis=-1):
    middle = jnp.mean(values, axis=axis, keepdims=True)
    centred = values - middle
    spread = jnp.mean(centred * centred, axis=axis, keepdims=True)
    return centred * lax.rsqrt(spread + EPS) * gain + shift


def sigmoid(x):
    return 0.5 * jnp.tanh(0.5 * x) + 0.5


def call(kernel, out_shape, scratch, specs, cost=None, mib=24):
    return pl.pallas_call(
        kernel,
        out_shape=out_shape,
        in_specs=specs,
        out_specs=jax.tree.map(lambda _: VMEM, out_shape),
        scratch_shapes=scratch,
        compiler_params=pltpu.CompilerParams(vmem_limit_bytes=mib * 1024 * 1024),
        cost_estimate=cost,
    )


def struct(shape, dtype=BF16):
    return jax.ShapeDtypeStruct(shape, dtype)


def turn_kernel(pair_ref, out_ref, wide):
    wide[...] = pair_ref[...].astype(F32).reshape(RI * CJ, C)
    for j in range(CJ):
        out_ref[j] = wide[pl.ds(j, RI, stride=CJ), :].astype(BF16)


def turn_back_kernel(in_ref, out_ref, wide):
    for j in range(CJ):
        wide[pl.ds(j, RI, stride=CJ), :] = in_ref[j].astype(F32)
    out_ref[...] = wide[...].reshape(RI, CJ, C).astype(BF16)


def column(ref, t):
    return jnp.concatenate([ref[r * T + t] for r in range(ROWS)], axis=0)


def project_kernel(x_ref, valid_t_ref, valid_ref, norms_ref, w_ref, out_ref, wide):
    wide[...] = jnp.zeros_like(wide)
    for t in range(T):
        x = column(x_ref, t).astype(F32)
        normed = layer_norm(x, norms_ref[0:1], norms_ref[1:2]).astype(BF16)
        proj = dot(w_ref[...], normed, ((1,), (1,)))
        mask = valid_ref[...] * valid_t_ref[t]
        for side in range(2):
            gate = proj[2 * side * C : (2 * side + 1) * C]
            value = proj[(2 * side + 1) * C : (2 * side + 2) * C]
            part = mask * sigmoid(gate) * value
            for l in range(L):
                wide[pl.ds(side * T * L + t * L + l, C, stride=SEND), :] = part[
                    :, l * C : (l + 1) * C
                ]
    out_ref[...] = wide[...].reshape(C, SEND, C).astype(BF16)


def gate_kernel(x_ref, norms_ref, w_ref, out_ref):
    for t in range(T):
        x = column(x_ref, t).astype(F32)
        normed = layer_norm(x, norms_ref[0:1], norms_ref[1:2]).astype(BF16)
        out_ref[t] = sigmoid(dot(normed, w_ref[...], ((1,), (0,))))


def product_kernel(in_ref, out_ref, wide, left, right, prod, back):
    wide[...] = in_ref[...].astype(F32).reshape(C * SEND, C)
    for t in range(T):
        for l in range(L):
            left[t * C : (t + 1) * C, l * C : (l + 1) * C] = wide[
                pl.ds(t * L + l, C, stride=SEND), :
            ].astype(BF16)
            right[t * C : (t + 1) * C, l * C : (l + 1) * C] = wide[
                pl.ds(T * L + t * L + l, C, stride=SEND), :
            ].astype(BF16)
    back[...] = jnp.zeros_like(back)
    for l in range(L):
        prod[l] = dot(right[...], left[:, l * C : (l + 1) * C], ((0,), (0,)))
        for t in range(T):
            back[pl.ds(t * L + l, C, stride=BACK), :] = prod[l, pl.ds(t, C, stride=T), :]
    out_ref[...] = back[...].reshape(C, BACK, C).astype(BF16)


def middle_kernel(
    in_ref, x_ref, gate_ref, norms_ref, w_ref,
    mid_ref, att_ref, pay_ref, wide, pay,
):
    wide[...] = in_ref[...].astype(F32).reshape(C * BACK, C)
    gain = jnp.broadcast_to(norms_ref[2:3], (C, C)).T[:, :1]
    bias = jnp.broadcast_to(norms_ref[3:4], (C, C)).T[:, :1]
    for t in range(T):
        prod = jnp.concatenate(
            [wide[pl.ds(t * L + l, C, stride=BACK), :] for l in range(L)], axis=1
        )
        normed = layer_norm(prod, gain, bias, 0).astype(BF16)
        update = dot(normed, w_ref[:C], ((0,), (0,)))
        mid = (column(x_ref, t).astype(F32) + gate_ref[t] * update).astype(BF16)
        att = layer_norm(mid.astype(F32), norms_ref[4:5], norms_ref[5:6]).astype(BF16)
        mid_ref[t] = mid
        att_ref[t] = att
        rows = dot(w_ref[C:], att, ((1,), (1,)))
        for h in range(H):
            pay[h * T + t : h * T + t + 1, :] = rows[h : h + 1]
    pay[H * T : PAY, :] = jnp.zeros((PAY - H * T, N), F32)
    for r in range(ROWS):
        pay_ref[r] = pay[...].astype(BF16)


def qkvg_kernel(att_ref, wqvg_ref, wk_ref, q_ref, k_ref, v_ref, g_ref):
    for t in range(T):
        att = att_ref[t]
        qvg = dot(att, wqvg_ref[...], ((1,), (0,)))
        q_ref[t] = (qvg[:, :C] * DH ** (-0.5)).astype(BF16)
        v_ref[t] = jnp.concatenate(
            [qvg[:, C : 2 * C].astype(BF16), jnp.ones((N, C), BF16)], axis=1
        )
        g_ref[t] = sigmoid(qvg[:, 2 * C :])
        k_ref[t] = dot(wk_ref[...], att, ((1,), (1,))).astype(BF16)


def merge_kernel(spread_ref, in_ref, out_ref):
    rows = in_ref[...].astype(F32).reshape(ROWS * PAY, N).astype(BF16)
    out_ref[...] = dot(spread_ref[...], rows, ((1,), (0,))).astype(BF16)


def attend_kernel(
    steps, me_ref, inter_ref, q_ref, k_ref, v_ref, g_ref, mid_ref, cross_ref, key_ref, valid_ref, valid_t_ref, wo_ref,
    *refs,
):
    parts, (out_ref, extra, score_a, score_b, power_a, power_b) = refs[:4], refs[4:]
    score, power = (score_a, score_b), (power_a, power_b)
    me = me_ref[0]
    chips = [(me // 2) ^ step for step in steps]
    for n in range(GROUP):
        for other in range(2):
            core = (me % 2) ^ other
            first = chips[n] * RI + core * CJ
            part = parts[2 * other] if n == 0 else parts[2 * other + 1].at[n - 1]
            for s in range(CJ // 8):
                to = pl.multiple_of(n * RI + core * CJ + 8 * s, 8)
                crossing = cross_ref[pl.ds((first + 8 * s) // MB, 1), :]
                for h in range(H):
                    extra[h, pl.ds(to, 8), :] = (
                        part[h * CJ + 8 * s : h * CJ + 8 * s + 8, :].astype(F32)
                        + inter_ref[h] * crossing
                        + key_ref[...]
                    )
    lane_head = lax.broadcasted_iota(jnp.int32, (CHUNK, C), 1) // DH

    def rows_of(take):
        return jnp.concatenate([take(pl.ds(pl.multiple_of(chip * RI, RI), RI)) for chip in chips], axis=0)

    valid = rows_of(lambda rows: valid_ref[rows, :])

    def one_column(t, carry):
        queries = rows_of(lambda rows: q_ref[t, rows, :])

        def set_score(h):
            own = jnp.where(lane_head == h, queries, jnp.zeros_like(queries))
            score[h % 2][...] = dot(own, k_ref[t], ((1,), (0,))) + extra[h]

        total = jnp.zeros((CHUNK, C), F32)
        set_score(0)
        for h in range(H):
            if h + 1 < H:
                set_score(h + 1)
            now = score[h % 2][...]
            highest = jnp.max(now, axis=1, keepdims=True)
            power[h % 2][...] = jnp.exp(now - highest).astype(BF16)
            sums = dot(power[h % 2][...], v_ref[t], ((1,), (0,)))
            total = jnp.where(lane_head == h, sums[:, :C] / sums[:, C:], total)
        gated = (rows_of(lambda rows: g_ref[t, rows, :]) * total).astype(BF16)
        update = dot(gated, wo_ref[...], ((1,), (0,)))
        mid = rows_of(lambda rows: mid_ref[t, rows, :]).astype(F32)
        out = (mid + valid * valid_t_ref[t] * update).astype(BF16)
        for n in range(GROUP):
            out_ref[n * T + t] = out[n * RI : (n + 1) * RI]
        return carry

    lax.fori_loop(0, T, one_column, 0)


def order_kernel(me_ref, *refs):
    out_ref = refs[-1]
    for step in range(ROWS):
        chip = (me_ref[0] // 2) ^ step
        for t in range(T):
            out_ref[chip * T + t] = refs[step % 2][step // 2 * T + t]


def on_device(
    pair,
    block_chain,
    block_valid,
    tri_norm_gain,
    tri_norm_bias,
    tri_in_weight,
    tri_gate_weight,
    out_norm_gain,
    out_norm_bias,
    tri_out_weight,
    att_norm_gain,
    att_norm_bias,
    qkvg_weight,
    bias_weight,
    inter_chain,
    att_out_weight,
):
    row_at, col_at = lax.axis_index("row"), lax.axis_index("col")
    residue_valid = jnp.repeat(block_valid, MB).astype(F32)
    residue_chain = jnp.repeat(block_chain, MB)
    valid_t = lax.dynamic_slice_in_dim(residue_valid, (col_at * ROWS + row_at) * T, T)
    valid_lanes = residue_valid[None, :]
    valid_rows = jnp.broadcast_to(residue_valid[:, None], (N, C))
    cross = (block_chain[:, None] != residue_chain[None, :]).astype(F32)
    key_mask = (MASK_NEG * (residue_valid - 1.0))[None, :]
    norms = jnp.stack(
        [tri_norm_gain, tri_norm_bias, out_norm_gain, out_norm_bias, att_norm_gain, att_norm_bias]
    )

    turned = call(turn_kernel, struct((CJ, RI, C)), [pltpu.VMEM((RI * CJ, C), F32)], [VMEM])(pair)
    x = lax.all_to_all(turned, "row", 0, 0, tiled=True)

    parcels = call(
        project_kernel,
        struct((C, SEND, C)),
        [pltpu.VMEM((C * SEND, C), F32)],
        [VMEM, SMEM, VMEM, VMEM, VMEM],
    )(x, valid_t, valid_lanes, norms, tri_in_weight.T)
    gate = call(gate_kernel, struct((T, N, C), F32), [], [VMEM] * 3)(
        x, norms, tri_gate_weight
    )
    channel = lax.all_to_all(parcels, ("col", "row"), 0, 0, tiled=True)
    product = call(
        product_kernel,
        struct((C, BACK, C)),
        [
            pltpu.VMEM((C * SEND, C), F32),
            pltpu.VMEM((N, N), BF16),
            pltpu.VMEM((N, N), BF16),
            pltpu.VMEM((L, N, C), F32),
            pltpu.VMEM((C * BACK, C), F32),
        ],
        [VMEM],
    )(channel)
    returned = lax.all_to_all(product, ("col", "row"), 0, 0, tiled=True)

    w_mid = jnp.concatenate([tri_out_weight, jnp.pad(bias_weight.T, ((0, 8 - H), (0, 0)))])
    mid, att, pay = call(
        middle_kernel,
        [struct((T, N, C)), struct((T, N, C)), struct((ROWS, PAY, N))],
        [pltpu.VMEM((C * BACK, C), F32), pltpu.VMEM((PAY, N), F32)],
        [VMEM] * 5,
    )(
        returned, x, gate, norms, w_mid
    )

    both = ("row", "col")

    def swap(values, row_xor, col_xor):
        pairs = [
            (r * COLS + c, (r ^ row_xor) * COLS + (c ^ col_xor))
            for r in range(ROWS)
            for c in range(COLS)
        ]
        return lax.ppermute(values, both, pairs)

    wanted = jnp.arange(H * CJ)
    head, part, t = wanted // CJ, wanted % CJ // T, wanted % T
    spread = (
        (part * PAY + head * T + t)[:, None] == jnp.arange(ROWS * PAY)[None, :]
    ).astype(BF16)
    merged = call(merge_kernel, struct((H * CJ, N)), [], [VMEM] * 2)(
        spread, lax.all_to_all(pay, "row", 0, 0, tiled=True)
    )
    hold = lax.optimization_barrier
    *column, beside = hold([swap(merged, 0, 4 * d) for d in range(1, GROUP)] + [swap(merged, 0, 2)])
    along = jnp.stack(column)
    across = swap(along, 0, 2)
    wqvg = jnp.concatenate([qkvg_weight[:, :C], qkvg_weight[:, 2 * C :]], axis=1)
    q, k, v, g = call(
        qkvg_kernel,
        [struct((T, N, C)), struct((T, C, N)), struct((T, N, 2 * C)), struct((T, N, C), F32)],
        [],
        [VMEM] * 3,
    )(att, wqvg, qkvg_weight[:, C : 2 * C].T)


    def attend(first, *parts):
        steps = [2 * d + first for d in range(GROUP)]
        return call(
            functools.partial(attend_kernel, tuple(steps)),
            struct((GROUP * T, RI, C)),
            [pltpu.VMEM((H, CHUNK, N), F32)]
            + [pltpu.VMEM((CHUNK, N), F32)] * 2
            + [pltpu.VMEM((CHUNK, N), BF16)] * 2,
            [SMEM, SMEM] + [VMEM] * 8 + [SMEM, VMEM] + [VMEM] * 4,
            pl.CostEstimate(
                flops=2 * T * H * CHUNK * N * 3 * C,
                bytes_accessed=8 * 1024 * 1024,
                transcendentals=T * H * CHUNK * N,
            ),
        )(
            col_at[None], inter_chain, q, k, v, g, mid, cross, key_mask, valid_rows, valid_t, att_out_weight,
            *parts,
        )

    merged2, along2, beside2, q, k, v, g = hold(
        (swap(merged, 0, 1), swap(along, 0, 1), swap(beside, 0, 1), q, k, v, g)
    )
    near = attend(0, merged, along, merged2, along2)
    near, across = hold((near, across))
    far = attend(1, beside, across, beside2, swap(across, 0, 1))
    out = call(order_kernel, struct((CJ, RI, C)), [], [SMEM] + [VMEM] * 2)(col_at[None], near, far)
    home = lax.all_to_all(out, "row", 0, 0, tiled=True)
    return call(turn_back_kernel, struct((RI, CJ, C)), [pltpu.VMEM((RI * CJ, C), F32)], [VMEM])(home)


def solution(mesh):
    placed = (P("row", "col", None),) + (P(),) * 15
    return jax.shard_map(
        on_device, mesh=mesh, in_specs=placed, out_specs=P("row", "col", None), check_vma=False
    )
```

```python
import functools

import jax
import jax.numpy as jnp
from jax import lax
from jax.experimental import pallas as pl
from jax.experimental.pallas import tpu as pltpu
from jax.sharding import PartitionSpec as P

H = 4
DH = 32
MB = 64
C = 128
N = 640
ROWS = 8
COLS = 16
RI = N // ROWS
CJ = N // COLS
T = CJ // ROWS
SEND = 56
BACK = 32
G = RI // 16
A = CJ // 8
TURN = T * RI
PAY = 112
GROUP = 2
CHUNK = GROUP * RI

MASK_NEG = 10000.0
EPS = 1e-05

F32 = jnp.float32
BF16 = jnp.bfloat16
VMEM = pl.BlockSpec(memory_space=pltpu.VMEM)
SMEM = pl.BlockSpec(memory_space=pltpu.SMEM)


def dot(a, b, over):
    return lax.dot_general(a, b, (over, ((), ())), preferred_element_type=F32)


def layer_norm(values, gain, shift, axis=-1):
    middle = jnp.mean(values, axis=axis, keepdims=True)
    centred = values - middle
    spread = jnp.mean(centred * centred, axis=axis, keepdims=True)
    return centred * lax.rsqrt(spread + EPS) * gain + shift


def sigmoid(x):
    return 0.5 * jnp.tanh(0.5 * x) + 0.5


def call(kernel, out_shape, scratch, specs, cost=None, mib=24):
    return pl.pallas_call(
        kernel,
        out_shape=out_shape,
        in_specs=specs,
        out_specs=jax.tree.map(lambda _: VMEM, out_shape),
        scratch_shapes=scratch,
        compiler_params=pltpu.CompilerParams(vmem_limit_bytes=mib * 1024 * 1024),
        cost_estimate=cost,
    )


def struct(shape, dtype=BF16):
    return jax.ShapeDtypeStruct(shape, dtype)


def swap_groups(arrays):
    arrays = list(arrays)
    group = lax.broadcasted_iota(jnp.int32, arrays[0].shape, 1) // 16
    for bit in (1, 2, 4):
        high = (group & bit) != 0
        for p in range(8):
            if not p & bit:
                one, two = arrays[p], arrays[p | bit]
                arrays[p] = jnp.where(high, pltpu.roll(two, 16 * bit, 1), one)
                arrays[p | bit] = jnp.where(high, two, pltpu.roll(one, C - 16 * bit, 1))
    return arrays


def turn_back_kernel(in_ref, out_ref, wide):
    for j in range(CJ):
        wide[pl.ds(j, RI, stride=CJ), :] = in_ref[j].astype(F32)
    out_ref[...] = wide[...].reshape(RI, CJ, C).astype(BF16)


def project_kernel(
    pair_hbm, valid_hbm, gain_hbm, bias_hbm, w_hbm, out_ref, x_ref,
    pair_ref, valid_ref, gain_ref, bias_ref, w_ref, pairs, wide, sems,
):
    copies = [
        pltpu.make_async_copy(source, target, sems.at[n])
        for n, (source, target) in enumerate(
            (
                (pair_hbm, pair_ref),
                (valid_hbm, valid_ref),
                (gain_hbm, gain_ref),
                (bias_hbm, bias_ref),
                (w_hbm, w_ref),
            )
        )
    ]
    for copy in copies:
        copy.start()
    wide[...] = jnp.zeros_like(wide)
    for copy in copies:
        copy.wait()
    pairs[...] = pair_ref[...].astype(F32).reshape(RI * CJ, C)
    weight = w_ref[...].T
    for a in range(A):
        x = jnp.concatenate(
            [
                pairs[pl.ds(16 * g * CJ + 8 * a + b, 16, stride=CJ), :]
                for g in range(G)
                for b in range(8)
            ],
            axis=0,
        )
        x_ref[a] = x.astype(BF16)
        normed = layer_norm(x, gain_ref[...][None, :], bias_ref[...][None, :]).astype(BF16)
        proj = dot(weight, normed, ((1,), (1,)))
        valid_j = valid_ref[(lax.axis_index("col") * A + a) // (MB // 8)]
        for g in range(G):
            lanes = slice(g * C, (g + 1) * C)
            mask = (valid_ref[(lax.axis_index("row") * G + g) // (MB // 16)] * valid_j).astype(F32)
            for side in range(2):
                gate = proj[2 * side * C : (2 * side + 1) * C, lanes]
                value = proj[(2 * side + 1) * C : (2 * side + 2) * C, lanes]
                wide[pl.ds((side * A + a) * G + g, C, stride=SEND), :] = mask * sigmoid(gate) * value
    out_ref[...] = wide[...].reshape(C, SEND, C).astype(BF16)


def gate_kernel(x_ref, norms_ref, w_ref, out_ref):
    for a in range(A):
        x = x_ref[a].astype(F32)
        normed = layer_norm(x, norms_ref[0:1], norms_ref[1:2]).astype(BF16)
        out_ref[a] = sigmoid(dot(normed, w_ref[...], ((1,), (0,))))


def product_kernel(in_ref, out_ref, wide, left, right, prod, back):
    wide[...] = in_ref[...].astype(F32).reshape(C * SEND, C)
    for side, matrix in enumerate((left, right)):
        for a in range(A):
            rows = [
                wide[pl.ds((side * A + a) * G + g, C, stride=SEND), :].astype(BF16) for g in range(G)
            ]
            parts = swap_groups(
                [
                    jnp.concatenate([row[r * COLS : (r + 1) * COLS] for row in rows], axis=0)
                    for r in range(ROWS)
                ]
            )
            for b in range(8):
                first = (a * 8 + b) * COLS
                for g in range(G):
                    matrix[first : first + COLS, g * C : (g + 1) * C] = parts[b][
                        g * COLS : (g + 1) * COLS
                    ]
    back[...] = jnp.zeros_like(back)
    for g in range(G):
        prod[g] = dot(right[...], left[:, g * C : (g + 1) * C], ((0,), (0,)))
    for g in range(G):
        for half in range(2):
            firsts = [s // 2 * C + s % 2 * 8 for s in range(half * A, half * A + A)]
            parts = swap_groups(
                [
                    jnp.concatenate(
                        [prod[g, pl.ds(first + b, ROWS, stride=16), :] for first in firsts], axis=0
                    )
                    for b in range(8)
                ]
            )
            for r in range(ROWS):
                for a in range(A):
                    row = (r * COLS + half) * BACK + a * G + g
                    back[pl.ds(row, ROWS, stride=2 * BACK), :] = parts[r][a * ROWS : (a + 1) * ROWS]
    out_ref[...] = back[...].reshape(C, BACK, C).astype(BF16)


def middle_kernel(in_ref, x_ref, gate_ref, norms_ref, w_ref, out_ref, wide, pay):
    wide[...] = in_ref[...].astype(F32).reshape(C * BACK, C)
    pay[...] = jnp.zeros_like(pay)
    gain = jnp.broadcast_to(norms_ref[2:3], (C, C)).T[:, :1]
    bias = jnp.broadcast_to(norms_ref[3:4], (C, C)).T[:, :1]
    for a in range(A):
        prod = jnp.concatenate(
            [wide[pl.ds(a * G + g, C, stride=BACK), :] for g in range(G)], axis=1
        )
        normed = layer_norm(prod, gain, bias, 0).astype(BF16)
        update = dot(normed, w_ref[:C], ((0,), (0,)))
        mid = (x_ref[a].astype(F32) + gate_ref[a] * update).astype(BF16)
        for g in range(G):
            for b in range(8):
                r, t = divmod(8 * a + b, T)
                out_ref[r, t * RI + 16 * g : t * RI + 16 * g + 16, :] = mid[
                    (g * 8 + b) * 16 : (g * 8 + b + 1) * 16
                ]
        att = layer_norm(mid.astype(F32), norms_ref[4:5], norms_ref[5:6]).astype(BF16)
        rows = dot(w_ref[C:], att, ((1,), (1,)))
        for g in range(G):
            first = (a * G + g) * H
            pay[first : first + H, :] = rows[:H, g * C : (g + 1) * C]
    for r in range(ROWS):
        out_ref[r, TURN:, :] = pay[...].astype(BF16)


def qkvg_kernel(in_ref, norms_ref, wqg_ref, wv_ref, wk_ref, q_ref, k_ref, v_ref, g_ref):
    for t in range(T):
        mid = jnp.concatenate([in_ref[r, t * RI : (t + 1) * RI, :] for r in range(ROWS)], axis=0)
        att = layer_norm(mid.astype(F32), norms_ref[4:5], norms_ref[5:6]).astype(BF16)
        keyed = jnp.concatenate(
            [att[r * RI + 16 * g : r * RI + 16 * g + 16] for g in range(G) for r in range(ROWS)], axis=0
        )
        qg = dot(att, wqg_ref[...], ((1,), (0,)))
        q_ref[t] = (qg[:, :C] * DH ** (-0.5)).astype(BF16)
        g_ref[t] = sigmoid(qg[:, C:])
        vals = dot(keyed, wv_ref[...], ((1,), (0,))).astype(BF16)
        v_ref[t] = jnp.concatenate([vals, jnp.ones((N, C), BF16)], axis=1)
        k_ref[t] = dot(wk_ref[...], keyed, ((1,), (1,))).astype(BF16)


def merge_kernel(in_ref, out_ref, parts, rows):
    for b, part in enumerate(swap_groups([in_ref[r, TURN:, :].astype(F32) for r in range(ROWS)])):
        parts[b] = part
    for b in range(8):
        for g in range(G):
            for h in range(H):
                rows[g, pl.ds(h * CJ + b, A, stride=8), :] = parts[b, pl.ds(g * H + h, A, stride=G * H), :]
    out_ref[...] = jnp.concatenate([rows[g] for g in range(G)], axis=1).astype(BF16)


def attend_kernel(
    steps, me_ref, inter_ref, q_ref, k_ref, v_ref, g_ref, mid_ref, cross_ref, key_ref, valid_ref, valid_t_ref, wo_ref,
    *refs,
):
    parts, (out_ref, extra, score_a, score_b, power_a, power_b) = refs[: 2 * GROUP], refs[2 * GROUP :]
    score, power = (score_a, score_b), (power_a, power_b)
    me = me_ref[0]
    chips = [(me // 2) ^ step for step in steps]
    for n in range(GROUP):
        for other in range(2):
            core = (me % 2) ^ other
            first = chips[n] * RI + core * CJ
            part = parts[other * GROUP + n]
            for s in range(CJ // 8):
                to = pl.multiple_of(n * RI + core * CJ + 8 * s, 8)
                crossing = cross_ref[pl.ds((first + 8 * s) // MB, 1), :]
                for h in range(H):
                    extra[h, pl.ds(to, 8), :] = (
                        part[h * CJ + 8 * s : h * CJ + 8 * s + 8, :].astype(F32)
                        + inter_ref[h] * crossing
                        + key_ref[...]
                    )
    lane_head = lax.broadcasted_iota(jnp.int32, (CHUNK, C), 1) // DH

    def rows_of(take):
        return jnp.concatenate([take(pl.ds(pl.multiple_of(chip * RI, RI), RI)) for chip in chips], axis=0)

    valid = rows_of(lambda rows: valid_ref[rows, :])

    def one_column(t, carry):
        queries = rows_of(lambda rows: q_ref[t, rows, :])

        def set_score(h):
            own = jnp.where(lane_head == h, queries, jnp.zeros_like(queries))
            score[h % 2][...] = dot(own, k_ref[t], ((1,), (0,))) + extra[h]

        total = jnp.zeros((CHUNK, C), F32)
        set_score(0)
        for h in range(H + 1):
            if h + 1 < H:
                set_score(h + 1)
            if h > 0:
                sums = dot(power[(h - 1) % 2][...], v_ref[t], ((1,), (0,)))
                total = jnp.where(lane_head == h - 1, sums[:, :C] / sums[:, C:], total)
            if h < H:
                now = score[h % 2][...]
                highest = jnp.max(now, axis=1, keepdims=True)
                power[h % 2][...] = jnp.exp(now - highest).astype(BF16)
        gated = (rows_of(lambda rows: g_ref[t, rows, :]) * total).astype(BF16)
        update = dot(gated, wo_ref[...], ((1,), (0,)))
        own = pl.ds(pl.multiple_of(t * RI, RI), RI)
        mid = jnp.concatenate([mid_ref[chip, own, :] for chip in chips], axis=0).astype(F32)
        out = (mid + valid * valid_t_ref[t] * update).astype(BF16)
        for n in range(GROUP):
            out_ref[n * T + t] = out[n * RI : (n + 1) * RI]
        return carry

    lax.fori_loop(0, T, one_column, 0)


def order_kernel(me_ref, *refs):
    out_ref = refs[-1]
    for step in range(ROWS):
        chip = (me_ref[0] // 2) ^ step
        for t in range(T):
            out_ref[chip * T + t] = refs[step % 2 * 2 + step // 4][step % 4 // 2 * T + t]


def on_device(
    pair,
    block_chain,
    block_valid,
    tri_norm_gain,
    tri_norm_bias,
    tri_in_weight,
    tri_gate_weight,
    out_norm_gain,
    out_norm_bias,
    tri_out_weight,
    att_norm_gain,
    att_norm_bias,
    qkvg_weight,
    bias_weight,
    inter_chain,
    att_out_weight,
):
    row_at, col_at = lax.axis_index("row"), lax.axis_index("col")
    both = ("row", "col")
    residue_valid = jnp.repeat(block_valid, MB).astype(F32)
    norms = jnp.stack(
        [tri_norm_gain, tri_norm_bias, out_norm_gain, out_norm_bias, att_norm_gain, att_norm_bias]
    )

    parcels, x = call(
        project_kernel,
        [struct((C, SEND, C)), struct((A, N, C))],
        [
            pltpu.VMEM((RI, CJ, C), BF16),
            pltpu.SMEM((N // MB,), jnp.int32),
            pltpu.VMEM((C,), F32),
            pltpu.VMEM((C,), F32),
            pltpu.VMEM((C, 4 * C), BF16),
            pltpu.VMEM((RI * CJ, C), F32),
            pltpu.VMEM((C * SEND, C), F32),
            pltpu.SemaphoreType.DMA((5,)),
        ],
        [pl.BlockSpec(memory_space=pl.ANY)] * 5,
        mib=60,
    )(pair, block_valid, tri_norm_gain, tri_norm_bias, tri_in_weight)
    gate = call(gate_kernel, struct((A, N, C), F32), [], [VMEM] * 3)(x, norms, tri_gate_weight)
    channel = lax.all_to_all(parcels, both, 0, 0, tiled=True)
    product = call(
        product_kernel,
        struct((C, BACK, C)),
        [
            pltpu.VMEM((C * SEND, C), F32),
            pltpu.VMEM((N, N), BF16),
            pltpu.VMEM((N, N), BF16),
            pltpu.VMEM((G, N, C), F32),
            pltpu.VMEM((C * BACK, C), F32),
        ],
        [VMEM],
    )(channel)
    returned = lax.all_to_all(product, both, 0, 0, tiled=True)

    w_mid = jnp.concatenate([tri_out_weight, jnp.pad(bias_weight.T, ((0, 8 - H), (0, 0)))])
    turned = call(
        middle_kernel,
        struct((ROWS, TURN + PAY, C)),
        [pltpu.VMEM((C * BACK, C), F32), pltpu.VMEM((PAY, C), F32)],
        [VMEM] * 5,
    )(returned, x, gate, norms, w_mid)
    mid = lax.all_to_all(turned, "row", 0, 0, tiled=True)

    valid_t = lax.dynamic_slice_in_dim(residue_valid, (col_at * ROWS + row_at) * T, T)
    valid_rows = jnp.broadcast_to(residue_valid[:, None], (N, C))

    def keyed(values):
        return values.reshape(ROWS, G, 16).transpose(1, 0, 2).reshape(N)

    cross = (block_chain[:, None] != keyed(jnp.repeat(block_chain, MB))[None, :]).astype(F32)
    key_mask = (MASK_NEG * (keyed(residue_valid) - 1.0))[None, :]

    def swap(values, row_xor, col_xor):
        pairs = [
            (r * COLS + c, (r ^ row_xor) * COLS + (c ^ col_xor))
            for r in range(ROWS)
            for c in range(COLS)
        ]
        return lax.ppermute(values, both, pairs)

    merged = call(
        merge_kernel,
        struct((H * CJ, N)),
        [pltpu.VMEM((ROWS, PAY, C), F32), pltpu.VMEM((G, H * CJ, C), F32)],
        [VMEM],
    )(mid)
    hold = lax.optimization_barrier
    one, two, three, beside = [swap(merged, 0, step) for step in (4, 8, 12, 2)]

    wqg = jnp.concatenate([qkvg_weight[:, :C], qkvg_weight[:, 3 * C :]], axis=1)
    q, k, v, g = call(
        qkvg_kernel,
        [struct((T, N, C)), struct((T, C, N)), struct((T, N, 2 * C)), struct((T, N, C), F32)],
        [],
        [VMEM] * 5,
    )(mid, norms, wqg, qkvg_weight[:, 2 * C : 3 * C], qkvg_weight[:, C : 2 * C].T)

    def attend(steps, *parts):
        return call(
            functools.partial(attend_kernel, tuple(steps)),
            struct((GROUP * T, RI, C)),
            [pltpu.VMEM((H, CHUNK, N), F32)]
            + [pltpu.VMEM((CHUNK, N), F32)] * 2
            + [pltpu.VMEM((CHUNK, N), BF16)] * 2,
            [SMEM, SMEM] + [VMEM] * 8 + [SMEM, VMEM] + [VMEM] * (2 * GROUP),
            pl.CostEstimate(flops=1 << 20, bytes_accessed=1 << 16, transcendentals=0),
        )(
            col_at[None], inter_chain, q, k, v, g, mid, cross, key_mask, valid_rows, valid_t, att_out_weight,
            *parts,
        )

    def core(values):
        return swap(values, 0, 1)

    one_across = swap(one, 0, 2)
    merged, near, merged2, near2, q, k, v, g = hold((merged, one, core(merged), core(one), q, k, v, g))
    outs = [attend((0, 2), merged, near, merged2, near2)]
    outs[0], two, three, beside, one_across = hold((outs[0], two, three, beside, one_across))
    two_across, three_across = swap(two, 0, 2), swap(three, 0, 2)
    two, three, two2, three2, beside2, one_across2 = hold(
        (two, three, core(two), core(three), core(beside), core(one_across))
    )
    outs.append(attend((4, 6), two, three, two2, three2))
    outs[1], two_across = hold((outs[1], two_across))
    two_across2 = core(two_across)
    outs.append(attend((1, 3), beside, one_across, beside2, one_across2))
    outs[2], three_across, two_across2 = hold((outs[2], three_across, two_across2))
    outs.append(attend((5, 7), two_across, three_across, two_across2, core(three_across)))
    out = call(order_kernel, struct((CJ, RI, C)), [], [SMEM] + [VMEM] * 4)(col_at[None], *outs)
    home = lax.all_to_all(out, "row", 0, 0, tiled=True)
    return call(turn_back_kernel, struct((RI, CJ, C)), [pltpu.VMEM((RI * CJ, C), F32)], [VMEM])(home)


def solution(mesh):
    placed = (P("row", "col", None),) + (P(),) * 15
    return jax.shard_map(
        on_device, mesh=mesh, in_specs=placed, out_specs=P("row", "col", None), check_vma=False
    )
```

```python
import functools
import math

import jax
import jax.numpy as jnp
from jax import lax
from jax.experimental import pallas as pl
from jax.experimental.pallas import tpu as pltpu
from jax.sharding import PartitionSpec as P

H = 4
DH = 32
MB = 64
C = 128
N = 640
ROWS = 8
COLS = 16
RI = N // ROWS
CJ = N // COLS
T = CJ // ROWS
SEND = 56
PITCH = 40
BACK = 32
G = RI // 16
A = CJ // 8
TURN = T * RI
PAY = 112
GROUP = 2
CHUNK = GROUP * RI

MASK_NEG = 10000.0
EPS = 1e-05
LOG2E = math.log2(math.e)

F32 = jnp.float32
BF16 = jnp.bfloat16
VMEM = pl.BlockSpec(memory_space=pltpu.VMEM)
SMEM = pl.BlockSpec(memory_space=pltpu.SMEM)


def dot(a, b, over):
    return lax.dot_general(a, b, (over, ((), ())), preferred_element_type=F32)


def layer_norm(values, gain, shift, axis=-1):
    middle = jnp.mean(values, axis=axis, keepdims=True)
    centred = values - middle
    spread = jnp.mean(centred * centred, axis=axis, keepdims=True)
    return centred * lax.rsqrt(spread + EPS) * gain + shift


def sigmoid(x):
    return 0.5 * jnp.tanh(0.5 * x) + 0.5


def call(kernel, out_shape, scratch, specs, cost=None, mib=24):
    return pl.pallas_call(
        kernel,
        out_shape=out_shape,
        in_specs=specs,
        out_specs=jax.tree.map(lambda _: VMEM, out_shape),
        scratch_shapes=scratch,
        compiler_params=pltpu.CompilerParams(vmem_limit_bytes=mib * 1024 * 1024),
        cost_estimate=cost,
    )


def struct(shape, dtype=BF16):
    return jax.ShapeDtypeStruct(shape, dtype)


def swap_groups(arrays):
    arrays = list(arrays)
    group = lax.broadcasted_iota(jnp.int32, arrays[0].shape, 1) // 16
    for bit in (1, 2, 4):
        high = (group & bit) != 0
        for p in range(8):
            if not p & bit:
                one, two = arrays[p], arrays[p | bit]
                arrays[p] = jnp.where(high, pltpu.roll(two, 16 * bit, 1), one)
                arrays[p | bit] = jnp.where(high, two, pltpu.roll(one, C - 16 * bit, 1))
    return arrays


def turn_back_kernel(in_ref, out_ref, wide):
    for j in range(CJ):
        wide[pl.ds(j, RI, stride=CJ), :] = in_ref[j].astype(F32)
    out_ref[...] = wide[...].reshape(RI, CJ, C).astype(BF16)


def project_kernel(
    pair_hbm, valid_hbm, gain_hbm, bias_hbm, w_hbm, out_ref, x_ref,
    pair_ref, valid_ref, gain_ref, bias_ref, w_ref, pairs, wide, sems,
):
    copies = [
        pltpu.make_async_copy(source, target, sems.at[n])
        for n, (source, target) in enumerate(
            (
                (pair_hbm, pair_ref),
                (valid_hbm, valid_ref),
                (gain_hbm, gain_ref),
                (bias_hbm, bias_ref),
                (w_hbm, w_ref),
            )
        )
    ]
    for copy in copies:
        copy.start()
    wide[...] = jnp.zeros_like(wide)
    for copy in copies:
        copy.wait()
    pairs[...] = pair_ref[...].astype(F32).reshape(RI * CJ, C)
    weight = w_ref[...].T
    for a in range(A):
        x = jnp.concatenate(
            [
                pairs[pl.ds(16 * g * CJ + 8 * a + b, 16, stride=CJ), :]
                for g in range(G)
                for b in range(8)
            ],
            axis=0,
        )
        x_ref[a] = x.astype(BF16)
        normed = layer_norm(x, gain_ref[...][None, :], bias_ref[...][None, :]).astype(BF16)
        proj = dot(weight, normed, ((1,), (1,)))
        valid_j = valid_ref[(lax.axis_index("col") * A + a) // (MB // 8)]
        for g in range(G):
            lanes = slice(g * C, (g + 1) * C)
            mask = (valid_ref[(lax.axis_index("row") * G + g) // (MB // 16)] * valid_j).astype(F32)
            for side in range(2):
                gate = proj[2 * side * C : (2 * side + 1) * C, lanes]
                value = proj[(2 * side + 1) * C : (2 * side + 2) * C, lanes]
                wide[pl.ds((side * A + a) * G + g, C, stride=SEND), :] = mask * sigmoid(gate) * value
    out_ref[...] = wide[...].reshape(C, SEND, C).astype(BF16)


def gate_kernel(x_ref, norms_ref, w_ref, out_ref):
    for a in range(A):
        x = x_ref[a].astype(F32)
        normed = layer_norm(x, norms_ref[0:1], norms_ref[1:2]).astype(BF16)
        out_ref[a] = sigmoid(dot(normed, w_ref[...], ((1,), (0,))))


def product_kernel(in_ref, out_ref, wide, left, right, prod, back):
    wide[...] = in_ref[...].astype(F32).reshape(C * SEND, C)
    for side, matrix in enumerate((left, right)):
        for a in range(A):
            rows = [
                wide[pl.ds((side * A + a) * G + g, C, stride=SEND), :].astype(BF16) for g in range(G)
            ]
            parts = swap_groups(
                [
                    jnp.concatenate([row[r * COLS : (r + 1) * COLS] for row in rows], axis=0)
                    for r in range(ROWS)
                ]
            )
            for b in range(8):
                first = (a * 8 + b) * COLS
                for g in range(G):
                    matrix[first : first + COLS, g * C : (g + 1) * C] = parts[b][
                        g * COLS : (g + 1) * COLS
                    ]
    back[...] = jnp.zeros_like(back)
    for g in range(G):
        prod[g] = dot(right[...], left[:, g * C : (g + 1) * C], ((0,), (0,)))
    for g in range(G):
        for half in range(2):
            firsts = [s // 2 * C + s % 2 * 8 for s in range(half * A, half * A + A)]
            parts = swap_groups(
                [
                    jnp.concatenate(
                        [prod[g, pl.ds(first + b, ROWS, stride=16), :] for first in firsts], axis=0
                    )
                    for b in range(8)
                ]
            )
            for r in range(ROWS):
                for a in range(A):
                    row = (r * COLS + half) * PITCH + a * G + g
                    back[pl.ds(row, ROWS, stride=2 * PITCH), :] = parts[r][a * ROWS : (a + 1) * ROWS]
    out_ref[...] = back[...].reshape(C, PITCH, C)[:, :BACK].astype(BF16)


def middle_kernel(in_ref, x_ref, gate_ref, norms_ref, w_ref, out_ref, wide, pay):
    wide[...] = in_ref[...].astype(F32).reshape(C * BACK, C)
    pay[...] = jnp.zeros_like(pay)
    gain = jnp.broadcast_to(norms_ref[2:3], (C, C)).T[:, :1]
    bias = jnp.broadcast_to(norms_ref[3:4], (C, C)).T[:, :1]
    for a in range(A):
        prod = jnp.concatenate(
            [wide[pl.ds(a * G + g, C, stride=BACK), :] for g in range(G)], axis=1
        )
        normed = layer_norm(prod, gain, bias, 0).astype(BF16)
        update = dot(normed, w_ref[:C], ((0,), (0,)))
        mid = (x_ref[a].astype(F32) + gate_ref[a] * update).astype(BF16)
        for g in range(G):
            for b in range(8):
                r, t = divmod(8 * a + b, T)
                out_ref[r, t * RI + 16 * g : t * RI + 16 * g + 16, :] = mid[
                    (g * 8 + b) * 16 : (g * 8 + b + 1) * 16
                ]
        att = layer_norm(mid.astype(F32), norms_ref[4:5], norms_ref[5:6]).astype(BF16)
        rows = dot(w_ref[C:], att, ((1,), (1,)))
        for g in range(G):
            first = (a * G + g) * H
            pay[first : first + H, :] = rows[:H, g * C : (g + 1) * C]
    for r in range(ROWS):
        out_ref[r, TURN:, :] = pay[...].astype(BF16)


def qkvg_kernel(in_ref, norms_ref, wqg_ref, wv_ref, wk_ref, q_ref, k_ref, v_ref, g_ref):
    lane_head = lax.broadcasted_iota(jnp.int32, (N, C), 1) // DH
    for t in range(T):
        mid = jnp.concatenate([in_ref[r, t * RI : (t + 1) * RI, :] for r in range(ROWS)], axis=0)
        att = layer_norm(mid.astype(F32), norms_ref[4:5], norms_ref[5:6]).astype(BF16)
        keyed = jnp.concatenate(
            [att[r * RI + 16 * g : r * RI + 16 * g + 16] for g in range(G) for r in range(ROWS)], axis=0
        )
        qg = dot(att, wqg_ref[...], ((1,), (0,)))
        q_ref[t] = (qg[:, :C] * (LOG2E * DH ** (-0.5))).astype(BF16)
        g_ref[t] = sigmoid(qg[:, C:])
        vals = dot(keyed, wv_ref[...], ((1,), (0,))).astype(BF16)
        for h in range(H):
            v_ref[t * H + h] = jnp.where(lane_head == h, vals, jnp.ones_like(vals))
        k_ref[t] = dot(wk_ref[...], keyed, ((1,), (1,))).astype(BF16)


def merge_kernel(in_ref, out_ref, parts, rows):
    for b, part in enumerate(swap_groups([in_ref[r, TURN:, :].astype(F32) for r in range(ROWS)])):
        parts[b] = part
    for b in range(8):
        for g in range(G):
            for h in range(H):
                rows[g, pl.ds(h * CJ + b, A, stride=8), :] = parts[b, pl.ds(g * H + h, A, stride=G * H), :]
    out_ref[...] = jnp.concatenate([rows[g] for g in range(G)], axis=1).astype(BF16)


def attend_kernel(
    steps, me_ref, inter_ref, q_ref, k_ref, v_ref, g_ref, mid_ref, cross_ref, key_ref, valid_ref, valid_t_ref, wo_ref,
    *refs,
):
    parts, (out_ref, extra, score_a, score_b, power_a, power_b) = refs[: 2 * GROUP], refs[2 * GROUP :]
    score, power = (score_a, score_b), (power_a, power_b)
    me = me_ref[0]
    chips = [(me // 2) ^ step for step in steps]
    for n in range(GROUP):
        for other in range(2):
            core = (me % 2) ^ other
            first = chips[n] * RI + core * CJ
            part = parts[other * GROUP + n]
            for s in range(CJ // 8):
                to = pl.multiple_of(n * RI + core * CJ + 8 * s, 8)
                crossing = cross_ref[pl.ds((first + 8 * s) // MB, 1), :]
                for h in range(H):
                    extra[h, pl.ds(to, 8), :] = LOG2E * (
                        part[h * CJ + 8 * s : h * CJ + 8 * s + 8, :].astype(F32)
                        + inter_ref[h] * crossing
                        + key_ref[...]
                    )
    lane_head = lax.broadcasted_iota(jnp.int32, (CHUNK, C), 1) // DH

    def rows_of(take):
        return jnp.concatenate([take(pl.ds(pl.multiple_of(chip * RI, RI), RI)) for chip in chips], axis=0)

    valid = rows_of(lambda rows: valid_ref[rows, :])

    def set_score(t, h):
        queries = rows_of(lambda rows: q_ref[t, rows, :])
        own = jnp.where(lane_head == h, queries, jnp.zeros_like(queries))
        score[h % 2][...] = dot(own, k_ref[t], ((1,), (0,))) + extra[h]

    def weigh(t, h, total):
        sums = dot(power[h % 2][...], v_ref[t * H + h], ((1,), (0,)))
        return jnp.where(lane_head == h, sums / pltpu.roll(sums, C // 2, 1), total)

    def finish(t, total):
        gated = (rows_of(lambda rows: g_ref[t, rows, :]) * total).astype(BF16)
        update = dot(gated, wo_ref[...], ((1,), (0,)))
        own = pl.ds(pl.multiple_of(t * RI, RI), RI)
        mid = jnp.concatenate([mid_ref[chip, own, :] for chip in chips], axis=0).astype(F32)
        out = (mid + valid * valid_t_ref[t] * update).astype(BF16)
        for n in range(GROUP):
            out_ref[n * T + t] = out[n * RI : (n + 1) * RI]

    def one_column(t, total):
        for h in range(H):
            if h + 1 < H:
                set_score(t, h + 1)
            else:
                set_score(jnp.minimum(t + 1, T - 1), 0)
            if h > 0:
                total = weigh(t, h - 1, total)
            else:
                before = jnp.maximum(t - 1, 0)
                finish(before, weigh(before, H - 1, total))
            now = score[h % 2][...]
            highest = jnp.max(now, axis=1, keepdims=True)
            power[h % 2][...] = jnp.exp2(now - highest).astype(BF16)
        return total

    power[(H - 1) % 2][...] = jnp.ones((CHUNK, N), BF16)
    set_score(0, 0)
    total = lax.fori_loop(0, T, one_column, jnp.zeros((CHUNK, C), F32))
    finish(T - 1, weigh(T - 1, H - 1, total))


def order_kernel(me_ref, *refs):
    out_ref = refs[-1]
    for step in range(ROWS):
        chip = (me_ref[0] // 2) ^ step
        for t in range(T):
            out_ref[chip * T + t] = refs[step % 2 * 2 + step // 4][step % 4 // 2 * T + t]


def on_device(
    pair,
    block_chain,
    block_valid,
    tri_norm_gain,
    tri_norm_bias,
    tri_in_weight,
    tri_gate_weight,
    out_norm_gain,
    out_norm_bias,
    tri_out_weight,
    att_norm_gain,
    att_norm_bias,
    qkvg_weight,
    bias_weight,
    inter_chain,
    att_out_weight,
):
    row_at, col_at = lax.axis_index("row"), lax.axis_index("col")
    both = ("row", "col")
    residue_valid = jnp.repeat(block_valid, MB).astype(F32)
    norms = jnp.stack(
        [tri_norm_gain, tri_norm_bias, out_norm_gain, out_norm_bias, att_norm_gain, att_norm_bias]
    )

    parcels, x = call(
        project_kernel,
        [struct((C, SEND, C)), struct((A, N, C))],
        [
            pltpu.VMEM((RI, CJ, C), BF16),
            pltpu.SMEM((N // MB,), jnp.int32),
            pltpu.VMEM((C,), F32),
            pltpu.VMEM((C,), F32),
            pltpu.VMEM((C, 4 * C), BF16),
            pltpu.VMEM((RI * CJ, C), F32),
            pltpu.VMEM((C * SEND, C), F32),
            pltpu.SemaphoreType.DMA((5,)),
        ],
        [pl.BlockSpec(memory_space=pl.ANY)] * 5,
        mib=60,
    )(pair, block_valid, tri_norm_gain, tri_norm_bias, tri_in_weight)
    gate = call(gate_kernel, struct((A, N, C), F32), [], [VMEM] * 3)(x, norms, tri_gate_weight)
    channel = lax.all_to_all(parcels, both, 0, 0, tiled=True)
    product = call(
        product_kernel,
        struct((C, BACK, C)),
        [
            pltpu.VMEM((C * SEND, C), F32),
            pltpu.VMEM((N, N), BF16),
            pltpu.VMEM((N, N), BF16),
            pltpu.VMEM((G, N, C), F32),
            pltpu.VMEM((C * PITCH, C), F32),
        ],
        [VMEM],
    )(channel)
    returned = lax.all_to_all(product, both, 0, 0, tiled=True)

    w_mid = jnp.concatenate([tri_out_weight, jnp.pad(bias_weight.T, ((0, 8 - H), (0, 0)))])
    turned = call(
        middle_kernel,
        struct((ROWS, TURN + PAY, C)),
        [pltpu.VMEM((C * BACK, C), F32), pltpu.VMEM((PAY, C), F32)],
        [VMEM] * 5,
    )(returned, x, gate, norms, w_mid)
    mid = lax.all_to_all(turned, "row", 0, 0, tiled=True)

    valid_t = lax.dynamic_slice_in_dim(residue_valid, (col_at * ROWS + row_at) * T, T)
    valid_rows = jnp.broadcast_to(residue_valid[:, None], (N, C))

    def keyed(values):
        return values.reshape(ROWS, G, 16).transpose(1, 0, 2).reshape(N)

    cross = (block_chain[:, None] != keyed(jnp.repeat(block_chain, MB))[None, :]).astype(F32)
    key_mask = (MASK_NEG * (keyed(residue_valid) - 1.0))[None, :]

    def swap(values, row_xor, col_xor):
        pairs = [
            (r * COLS + c, (r ^ row_xor) * COLS + (c ^ col_xor))
            for r in range(ROWS)
            for c in range(COLS)
        ]
        return lax.ppermute(values, both, pairs)

    merged = call(
        merge_kernel,
        struct((H * CJ, N)),
        [pltpu.VMEM((ROWS, PAY, C), F32), pltpu.VMEM((G, H * CJ, C), F32)],
        [VMEM],
    )(mid)
    hold = lax.optimization_barrier

    def core(values):
        return swap(values, 0, 1)

    one, merged2 = swap(merged, 0, 4), core(merged)
    wqg = jnp.concatenate([qkvg_weight[:, :C], qkvg_weight[:, 3 * C :]], axis=1)
    q, k, v, g = call(
        qkvg_kernel,
        [struct((T, N, C)), struct((T, C, N)), struct((T * H, N, C)), struct((T, N, C), F32)],
        [],
        [VMEM] * 5,
    )(mid, norms, wqg, qkvg_weight[:, 2 * C : 3 * C], qkvg_weight[:, C : 2 * C].T)

    merged, q, k, v, g = hold((merged, q, k, v, g))
    two, three, beside = [swap(merged, 0, step) for step in (8, 12, 2)]

    def attend(steps, *parts):
        return call(
            functools.partial(attend_kernel, tuple(steps)),
            struct((GROUP * T, RI, C)),
            [pltpu.VMEM((H, CHUNK, N), F32)]
            + [pltpu.VMEM((CHUNK, N), F32)] * 2
            + [pltpu.VMEM((CHUNK, N), BF16)] * 2,
            [SMEM, SMEM] + [VMEM] * 8 + [SMEM, VMEM] + [VMEM] * (2 * GROUP),
            pl.CostEstimate(flops=1 << 20, bytes_accessed=1 << 16, transcendentals=0),
        )(
            col_at[None], inter_chain, q, k, v, g, mid, cross, key_mask, valid_rows, valid_t, att_out_weight,
            *parts,
        )

    one_across = swap(one, 0, 2)
    near = hold((merged, one, merged2, core(one)))
    outs = [attend((0, 2), *near)]
    outs[0], two, three, beside = hold((outs[0], two, three, beside))
    two_across, three_across = swap(two, 0, 2), swap(three, 0, 2)
    two, three, two2, three2, beside2 = hold((two, three, core(two), core(three), core(beside)))
    outs.append(attend((4, 6), two, three, two2, three2))
    outs[1], one_across, two_across = hold((outs[1], one_across, two_across))
    two_across2 = core(two_across)
    outs.append(attend((1, 3), beside, one_across, beside2, core(one_across)))
    outs[2], three_across, two_across2 = hold((outs[2], three_across, two_across2))
    outs.append(attend((5, 7), two_across, three_across, two_across2, core(three_across)))
    out = call(order_kernel, struct((CJ, RI, C)), [], [SMEM] + [VMEM] * 4)(col_at[None], *outs)
    home = lax.all_to_all(out, "row", 0, 0, tiled=True)
    return call(turn_back_kernel, struct((RI, CJ, C)), [pltpu.VMEM((RI * CJ, C), F32)], [VMEM])(home)


def solution(mesh):
    placed = (P("row", "col", None),) + (P(),) * 15
    return jax.shard_map(
        on_device, mesh=mesh, in_specs=placed, out_specs=P("row", "col", None), check_vma=False
    )
```

```python
import functools

import jax
import jax.numpy as jnp
from jax import lax
from jax.experimental import pallas as pl
from jax.experimental.pallas import tpu as pltpu
from jax.sharding import PartitionSpec as P

H = 4
DH = 32
MB = 64
C = 128
N = 640
ROWS = 8
COLS = 16
RI = N // ROWS
CJ = N // COLS
T = CJ // ROWS
SEND = 56
BACK = 32
G = RI // 16
A = CJ // 8
TURN = T * RI
PAY = 112
GROUP = 2
CHUNK = GROUP * RI

MASK_NEG = 10000.0
EPS = 1e-05

F32 = jnp.float32
BF16 = jnp.bfloat16
VMEM = pl.BlockSpec(memory_space=pltpu.VMEM)
SMEM = pl.BlockSpec(memory_space=pltpu.SMEM)


def dot(a, b, over):
    return lax.dot_general(a, b, (over, ((), ())), preferred_element_type=F32)


def layer_norm(values, gain, shift, axis=-1):
    middle = jnp.mean(values, axis=axis, keepdims=True)
    centred = values - middle
    spread = jnp.mean(centred * centred, axis=axis, keepdims=True)
    return centred * lax.rsqrt(spread + EPS) * gain + shift


def sigmoid(x):
    return 0.5 * jnp.tanh(0.5 * x) + 0.5


def call(kernel, out_shape, scratch, specs, cost=None, mib=24):
    return pl.pallas_call(
        kernel,
        out_shape=out_shape,
        in_specs=specs,
        out_specs=jax.tree.map(lambda _: VMEM, out_shape),
        scratch_shapes=scratch,
        compiler_params=pltpu.CompilerParams(vmem_limit_bytes=mib * 1024 * 1024),
        cost_estimate=cost,
    )


def struct(shape, dtype=BF16):
    return jax.ShapeDtypeStruct(shape, dtype)


def swap_groups(arrays):
    arrays = list(arrays)
    group = lax.broadcasted_iota(jnp.int32, arrays[0].shape, 1) // 16
    for bit in (1, 2, 4):
        high = (group & bit) != 0
        for p in range(8):
            if not p & bit:
                one, two = arrays[p], arrays[p | bit]
                arrays[p] = jnp.where(high, pltpu.roll(two, 16 * bit, 1), one)
                arrays[p | bit] = jnp.where(high, two, pltpu.roll(one, C - 16 * bit, 1))
    return arrays


def turn_back_kernel(in_ref, out_ref, wide):
    for j in range(CJ):
        wide[pl.ds(j, RI, stride=CJ), :] = in_ref[j].astype(F32)
    out_ref[...] = wide[...].reshape(RI, CJ, C).astype(BF16)


def project_kernel(
    pair_hbm, valid_hbm, gain_hbm, bias_hbm, w_hbm, out_ref, x_ref,
    pair_ref, valid_ref, gain_ref, bias_ref, w_ref, pairs, wide, sems,
):
    copies = [
        pltpu.make_async_copy(source, target, sems.at[n])
        for n, (source, target) in enumerate(
            (
                (pair_hbm, pair_ref),
                (valid_hbm, valid_ref),
                (gain_hbm, gain_ref),
                (bias_hbm, bias_ref),
                (w_hbm, w_ref),
            )
        )
    ]
    for copy in copies:
        copy.start()
    wide[...] = jnp.zeros_like(wide)
    for copy in copies:
        copy.wait()
    pairs[...] = pair_ref[...].astype(F32).reshape(RI * CJ, C)
    weight = w_ref[...].T
    for a in range(A):
        x = jnp.concatenate(
            [
                pairs[pl.ds(16 * g * CJ + 8 * a + b, 16, stride=CJ), :]
                for g in range(G)
                for b in range(8)
            ],
            axis=0,
        )
        x_ref[a] = x.astype(BF16)
        normed = layer_norm(x, gain_ref[...][None, :], bias_ref[...][None, :]).astype(BF16)
        proj = dot(weight, normed, ((1,), (1,)))
        valid_j = valid_ref[(lax.axis_index("col") * A + a) // (MB // 8)]
        for g in range(G):
            lanes = slice(g * C, (g + 1) * C)
            mask = (valid_ref[(lax.axis_index("row") * G + g) // (MB // 16)] * valid_j).astype(F32)
            for side in range(2):
                gate = proj[2 * side * C : (2 * side + 1) * C, lanes]
                value = proj[(2 * side + 1) * C : (2 * side + 2) * C, lanes]
                wide[pl.ds((side * A + a) * G + g, C, stride=SEND), :] = mask * sigmoid(gate) * value
    out_ref[...] = wide[...].reshape(C, SEND, C).astype(BF16)


def gate_kernel(x_ref, norms_ref, w_ref, out_ref):
    for a in range(A):
        x = x_ref[a].astype(F32)
        normed = layer_norm(x, norms_ref[0:1], norms_ref[1:2]).astype(BF16)
        out_ref[a] = sigmoid(dot(normed, w_ref[...], ((1,), (0,))))


def product_kernel(in_ref, out_ref, wide, left, right, prod, back):
    wide[...] = in_ref[...].astype(F32).reshape(C * SEND, C)
    for side, matrix in enumerate((left, right)):
        for a in range(A):
            rows = [
                wide[pl.ds((side * A + a) * G + g, C, stride=SEND), :].astype(BF16) for g in range(G)
            ]
            parts = swap_groups(
                [
                    jnp.concatenate([row[r * COLS : (r + 1) * COLS] for row in rows], axis=0)
                    for r in range(ROWS)
                ]
            )
            for b in range(8):
                first = (a * 8 + b) * COLS
                for g in range(G):
                    matrix[first : first + COLS, g * C : (g + 1) * C] = parts[b][
                        g * COLS : (g + 1) * COLS
                    ]
    back[...] = jnp.zeros_like(back)
    for g in range(G):
        prod[g] = dot(right[...], left[:, g * C : (g + 1) * C], ((0,), (0,)))
    for g in range(G):
        for half in range(2):
            firsts = [s // 2 * C + s % 2 * 8 for s in range(half * A, half * A + A)]
            parts = swap_groups(
                [
                    jnp.concatenate(
                        [prod[g, pl.ds(first + b, ROWS, stride=16), :] for first in firsts], axis=0
                    )
                    for b in range(8)
                ]
            )
            for r in range(ROWS):
                for a in range(A):
                    row = (r * COLS + half) * BACK + a * G + g
                    back[pl.ds(row, ROWS, stride=2 * BACK), :] = parts[r][a * ROWS : (a + 1) * ROWS]
    out_ref[...] = back[...].reshape(C, BACK, C).astype(BF16)


def middle_kernel(in_ref, x_ref, gate_ref, norms_ref, w_ref, out_ref, wide, pay):
    wide[...] = in_ref[...].astype(F32).reshape(C * BACK, C)
    pay[...] = jnp.zeros_like(pay)
    gain = jnp.broadcast_to(norms_ref[2:3], (C, C)).T[:, :1]
    bias = jnp.broadcast_to(norms_ref[3:4], (C, C)).T[:, :1]
    for a in range(A):
        prod = jnp.concatenate(
            [wide[pl.ds(a * G + g, C, stride=BACK), :] for g in range(G)], axis=1
        )
        normed = layer_norm(prod, gain, bias, 0).astype(BF16)
        update = dot(normed, w_ref[:C], ((0,), (0,)))
        mid = (x_ref[a].astype(F32) + gate_ref[a] * update).astype(BF16)
        for g in range(G):
            for b in range(8):
                r, t = divmod(8 * a + b, T)
                out_ref[r, t * RI + 16 * g : t * RI + 16 * g + 16, :] = mid[
                    (g * 8 + b) * 16 : (g * 8 + b + 1) * 16
                ]
        att = layer_norm(mid.astype(F32), norms_ref[4:5], norms_ref[5:6]).astype(BF16)
        rows = dot(w_ref[C:], att, ((1,), (1,)))
        for g in range(G):
            first = (a * G + g) * H
            pay[first : first + H, :] = rows[:H, g * C : (g + 1) * C]
    for r in range(ROWS):
        out_ref[r, TURN:, :] = pay[...].astype(BF16)


def qkvg_kernel(in_ref, norms_ref, wqg_ref, wv_ref, wk_ref, q_ref, k_ref, v_ref, g_ref):
    for t in range(T):
        mid = jnp.concatenate([in_ref[r, t * RI : (t + 1) * RI, :] for r in range(ROWS)], axis=0)
        att = layer_norm(mid.astype(F32), norms_ref[4:5], norms_ref[5:6]).astype(BF16)
        keyed = jnp.concatenate(
            [att[r * RI + 16 * g : r * RI + 16 * g + 16] for g in range(G) for r in range(ROWS)], axis=0
        )
        qg = dot(att, wqg_ref[...], ((1,), (0,)))
        q_ref[t] = (qg[:, :C] * DH ** (-0.5)).astype(BF16)
        g_ref[t] = sigmoid(qg[:, C:])
        vals = dot(keyed, wv_ref[...], ((1,), (0,))).astype(BF16)
        v_ref[t] = jnp.concatenate([vals, jnp.ones((N, C), BF16)], axis=1)
        k_ref[t] = dot(wk_ref[...], keyed, ((1,), (1,))).astype(BF16)


def merge_kernel(in_ref, out_ref, parts, rows):
    for b, part in enumerate(swap_groups([in_ref[r, TURN:, :].astype(F32) for r in range(ROWS)])):
        parts[b] = part
    for b in range(8):
        for g in range(G):
            for h in range(H):
                rows[g, pl.ds(h * CJ + b, A, stride=8), :] = parts[b, pl.ds(g * H + h, A, stride=G * H), :]
    out_ref[...] = jnp.concatenate([rows[g] for g in range(G)], axis=1).astype(BF16)


def attend_kernel(
    steps, me_ref, inter_ref, q_ref, k_ref, v_ref, g_ref, mid_ref, cross_ref, key_ref, valid_ref, valid_t_ref, wo_ref,
    *refs,
):
    parts, (out_ref, extra, score_a, score_b, power_a, power_b) = refs[:-6], refs[-6:]
    score, power = (score_a, score_b), (power_a, power_b)
    me = me_ref[0]
    chips = [(me // 2) ^ step for step in steps]
    for n in range(GROUP):
        for other in range(2):
            core = (me % 2) ^ other
            first = chips[n] * RI + core * CJ
            part = parts[other].at[n] if len(parts) == 2 else parts[other * GROUP + n]
            for s in range(CJ // 8):
                to = pl.multiple_of(n * RI + core * CJ + 8 * s, 8)
                crossing = cross_ref[pl.ds((first + 8 * s) // MB, 1), :]
                for h in range(H):
                    extra[h, pl.ds(to, 8), :] = (
                        part[h * CJ + 8 * s : h * CJ + 8 * s + 8, :].astype(F32)
                        + inter_ref[h] * crossing
                        + key_ref[...]
                    )
    lane_head = lax.broadcasted_iota(jnp.int32, (CHUNK, C), 1) // DH

    def rows_of(take):
        return jnp.concatenate([take(pl.ds(pl.multiple_of(chip * RI, RI), RI)) for chip in chips], axis=0)

    valid = rows_of(lambda rows: valid_ref[rows, :])

    def one_column(t, carry):
        queries = rows_of(lambda rows: q_ref[t, rows, :])

        def set_score(h):
            own = jnp.where(lane_head == h, queries, jnp.zeros_like(queries))
            score[h % 2][...] = dot(own, k_ref[t], ((1,), (0,))) + extra[h]

        total = jnp.zeros((CHUNK, C), F32)
        set_score(0)
        for h in range(H + 1):
            if h + 1 < H:
                set_score(h + 1)
            if h > 0:
                sums = dot(power[(h - 1) % 2][...], v_ref[t], ((1,), (0,)))
                total = jnp.where(lane_head == h - 1, sums[:, :C] / sums[:, C:], total)
            if h < H:
                now = score[h % 2][...]
                highest = jnp.max(now, axis=1, keepdims=True)
                power[h % 2][...] = jnp.exp(now - highest).astype(BF16)
        gated = (rows_of(lambda rows: g_ref[t, rows, :]) * total).astype(BF16)
        update = dot(gated, wo_ref[...], ((1,), (0,)))
        own = pl.ds(pl.multiple_of(t * RI, RI), RI)
        mid = jnp.concatenate([mid_ref[chip, own, :] for chip in chips], axis=0).astype(F32)
        out = (mid + valid * valid_t_ref[t] * update).astype(BF16)
        for n in range(GROUP):
            out_ref[n * T + t] = out[n * RI : (n + 1) * RI]
        return carry

    lax.fori_loop(0, T, one_column, 0)


def order_kernel(me_ref, *refs):
    out_ref = refs[-1]
    for step in range(ROWS):
        chip = (me_ref[0] // 2) ^ step
        for t in range(T):
            out_ref[chip * T + t] = refs[step % 2 * 2 + step // 4][step % 4 // 2 * T + t]


def on_device(
    pair,
    block_chain,
    block_valid,
    tri_norm_gain,
    tri_norm_bias,
    tri_in_weight,
    tri_gate_weight,
    out_norm_gain,
    out_norm_bias,
    tri_out_weight,
    att_norm_gain,
    att_norm_bias,
    qkvg_weight,
    bias_weight,
    inter_chain,
    att_out_weight,
):
    row_at, col_at = lax.axis_index("row"), lax.axis_index("col")
    both = ("row", "col")
    residue_valid = jnp.repeat(block_valid, MB).astype(F32)
    norms = jnp.stack(
        [tri_norm_gain, tri_norm_bias, out_norm_gain, out_norm_bias, att_norm_gain, att_norm_bias]
    )

    parcels, x = call(
        project_kernel,
        [struct((C, SEND, C)), struct((A, N, C))],
        [
            pltpu.VMEM((RI, CJ, C), BF16),
            pltpu.SMEM((N // MB,), jnp.int32),
            pltpu.VMEM((C,), F32),
            pltpu.VMEM((C,), F32),
            pltpu.VMEM((C, 4 * C), BF16),
            pltpu.VMEM((RI * CJ, C), F32),
            pltpu.VMEM((C * SEND, C), F32),
            pltpu.SemaphoreType.DMA((5,)),
        ],
        [pl.BlockSpec(memory_space=pl.ANY)] * 5,
        mib=60,
    )(pair, block_valid, tri_norm_gain, tri_norm_bias, tri_in_weight)
    gate = call(gate_kernel, struct((A, N, C), F32), [], [VMEM] * 3)(x, norms, tri_gate_weight)
    channel = lax.all_to_all(parcels, both, 0, 0, tiled=True)
    product = call(
        product_kernel,
        struct((C, BACK, C)),
        [
            pltpu.VMEM((C * SEND, C), F32),
            pltpu.VMEM((N, N), BF16),
            pltpu.VMEM((N, N), BF16),
            pltpu.VMEM((G, N, C), F32),
            pltpu.VMEM((C * BACK, C), F32),
        ],
        [VMEM],
    )(channel)
    returned = lax.all_to_all(product, both, 0, 0, tiled=True)

    w_mid = jnp.concatenate([tri_out_weight, jnp.pad(bias_weight.T, ((0, 8 - H), (0, 0)))])
    turned = call(
        middle_kernel,
        struct((ROWS, TURN + PAY, C)),
        [pltpu.VMEM((C * BACK, C), F32), pltpu.VMEM((PAY, C), F32)],
        [VMEM] * 5,
    )(returned, x, gate, norms, w_mid)
    mid = lax.all_to_all(turned, "row", 0, 0, tiled=True)

    valid_t = lax.dynamic_slice_in_dim(residue_valid, (col_at * ROWS + row_at) * T, T)
    valid_rows = jnp.broadcast_to(residue_valid[:, None], (N, C))

    def keyed(values):
        return values.reshape(ROWS, G, 16).transpose(1, 0, 2).reshape(N)

    cross = (block_chain[:, None] != keyed(jnp.repeat(block_chain, MB))[None, :]).astype(F32)
    key_mask = (MASK_NEG * (keyed(residue_valid) - 1.0))[None, :]

    def swap(values, row_xor, col_xor):
        pairs = [
            (r * COLS + c, (r ^ row_xor) * COLS + (c ^ col_xor))
            for r in range(ROWS)
            for c in range(COLS)
        ]
        return lax.ppermute(values, both, pairs)

    merged = call(
        merge_kernel,
        struct((H * CJ, N)),
        [pltpu.VMEM((ROWS, PAY, C), F32), pltpu.VMEM((G, H * CJ, C), F32)],
        [VMEM],
    )(mid)
    hold = lax.optimization_barrier

    def core(values):
        return swap(values, 0, 1)

    one, merged2 = swap(merged, 0, 4), core(merged)
    wqg = jnp.concatenate([qkvg_weight[:, :C], qkvg_weight[:, 3 * C :]], axis=1)
    q, k, v, g = call(
        qkvg_kernel,
        [struct((T, N, C)), struct((T, C, N)), struct((T, N, 2 * C)), struct((T, N, C), F32)],
        [],
        [VMEM] * 5,
    )(mid, norms, wqg, qkvg_weight[:, 2 * C : 3 * C], qkvg_weight[:, C : 2 * C].T)

    merged, q, k, v, g = hold((merged, q, k, v, g))
    two, three, beside = [swap(merged, 0, step) for step in (8, 12, 2)]

    def attend(steps, *parts):
        return call(
            functools.partial(attend_kernel, tuple(steps)),
            struct((GROUP * T, RI, C)),
            [pltpu.VMEM((H, CHUNK, N), F32)]
            + [pltpu.VMEM((CHUNK, N), F32)] * 2
            + [pltpu.VMEM((CHUNK, N), BF16)] * 2,
            [SMEM, SMEM] + [VMEM] * 8 + [SMEM, VMEM] + [VMEM] * len(parts),
            pl.CostEstimate(flops=1 << 20, bytes_accessed=1 << 16, transcendentals=0),
        )(
            col_at[None], inter_chain, q, k, v, g, mid, cross, key_mask, valid_rows, valid_t, att_out_weight,
            *parts,
        )

    one_across = swap(one, ROWS // 2, 2)
    near = hold((merged, one, merged2, core(one)))
    outs = [attend((0, 2), *near)]
    outs[0], two, three, beside, one_across = hold((outs[0], two, three, beside, one_across))
    column, across = jnp.stack([two, three]), jnp.stack([beside, one_across])
    far = swap(column, ROWS // 2, 2)
    column, across, column2, across2 = hold((column, across, core(column), core(across)))
    outs.append(attend((4, 6), column, column2))
    outs[1], across = hold((outs[1], across))
    outs.append(attend((1, 3), across, across2))
    outs[2], far = hold((outs[2], far))
    outs.append(attend((5, 7), far, core(far)))
    out = call(order_kernel, struct((CJ, RI, C)), [], [SMEM] + [VMEM] * 4)(col_at[None], *outs)
    home = lax.all_to_all(out, "row", 0, 0, tiled=True)
    return call(turn_back_kernel, struct((RI, CJ, C)), [pltpu.VMEM((RI * CJ, C), F32)], [VMEM])(home)


def solution(mesh):
    placed = (P("row", "col", None),) + (P(),) * 15
    return jax.shard_map(
        on_device, mesh=mesh, in_specs=placed, out_specs=P("row", "col", None), check_vma=False
    )
```

```python
import functools

import jax
import jax.numpy as jnp
from jax import lax
from jax.experimental import pallas as pl
from jax.experimental.pallas import tpu as pltpu
from jax.sharding import PartitionSpec as P

H = 4
DH = 32
MB = 64
C = 128
N = 640
ROWS = 8
COLS = 16
RI = N // ROWS
CJ = N // COLS
T = CJ // ROWS
SEND = 56
BACK = 32
G = RI // 16
A = CJ // 8
TURN = T * RI
PAY = 112
CALLS = ((0, 2), (4, 6, 1, 3), (5, 7))

MASK_NEG = 10000.0
EPS = 1e-05

F32 = jnp.float32
BF16 = jnp.bfloat16
VMEM = pl.BlockSpec(memory_space=pltpu.VMEM)
SMEM = pl.BlockSpec(memory_space=pltpu.SMEM)


def dot(a, b, over):
    return lax.dot_general(a, b, (over, ((), ())), preferred_element_type=F32)


def layer_norm(values, gain, shift, axis=-1):
    middle = jnp.mean(values, axis=axis, keepdims=True)
    centred = values - middle
    spread = jnp.mean(centred * centred, axis=axis, keepdims=True)
    return centred * lax.rsqrt(spread + EPS) * gain + shift


def sigmoid(x):
    return 0.5 * jnp.tanh(0.5 * x) + 0.5


def call(kernel, out_shape, scratch, specs, cost=None, mib=24):
    return pl.pallas_call(
        kernel,
        out_shape=out_shape,
        in_specs=specs,
        out_specs=jax.tree.map(lambda _: VMEM, out_shape),
        scratch_shapes=scratch,
        compiler_params=pltpu.CompilerParams(vmem_limit_bytes=mib * 1024 * 1024),
        cost_estimate=cost,
    )


def struct(shape, dtype=BF16):
    return jax.ShapeDtypeStruct(shape, dtype)


def swap_groups(arrays):
    arrays = list(arrays)
    group = lax.broadcasted_iota(jnp.int32, arrays[0].shape, 1) // 16
    for bit in (1, 2, 4):
        high = (group & bit) != 0
        for p in range(8):
            if not p & bit:
                one, two = arrays[p], arrays[p | bit]
                arrays[p] = jnp.where(high, pltpu.roll(two, 16 * bit, 1), one)
                arrays[p | bit] = jnp.where(high, two, pltpu.roll(one, C - 16 * bit, 1))
    return arrays


def turn_back_kernel(in_ref, out_ref, wide):
    for j in range(CJ):
        wide[pl.ds(j, RI, stride=CJ), :] = in_ref[j].astype(F32)
    out_ref[...] = wide[...].reshape(RI, CJ, C).astype(BF16)


def project_kernel(
    pair_hbm, valid_hbm, gain_hbm, bias_hbm, w_hbm, out_ref, x_ref,
    pair_ref, valid_ref, gain_ref, bias_ref, w_ref, pairs, wide, sems,
):
    copies = [
        pltpu.make_async_copy(source, target, sems.at[n])
        for n, (source, target) in enumerate(
            (
                (pair_hbm, pair_ref),
                (valid_hbm, valid_ref),
                (gain_hbm, gain_ref),
                (bias_hbm, bias_ref),
                (w_hbm, w_ref),
            )
        )
    ]
    for copy in copies:
        copy.start()
    wide[...] = jnp.zeros_like(wide)
    for copy in copies:
        copy.wait()
    pairs[...] = pair_ref[...].astype(F32).reshape(RI * CJ, C)
    weight = w_ref[...].T
    for a in range(A):
        x = jnp.concatenate(
            [
                pairs[pl.ds(16 * g * CJ + 8 * a + b, 16, stride=CJ), :]
                for g in range(G)
                for b in range(8)
            ],
            axis=0,
        )
        x_ref[a] = x.astype(BF16)
        normed = layer_norm(x, gain_ref[...][None, :], bias_ref[...][None, :]).astype(BF16)
        proj = dot(weight, normed, ((1,), (1,)))
        valid_j = valid_ref[(lax.axis_index("col") * A + a) // (MB // 8)]
        for g in range(G):
            lanes = slice(g * C, (g + 1) * C)
            mask = (valid_ref[(lax.axis_index("row") * G + g) // (MB // 16)] * valid_j).astype(F32)
            for side in range(2):
                gate = proj[2 * side * C : (2 * side + 1) * C, lanes]
                value = proj[(2 * side + 1) * C : (2 * side + 2) * C, lanes]
                wide[pl.ds((side * A + a) * G + g, C, stride=SEND), :] = mask * sigmoid(gate) * value
    out_ref[...] = wide[...].reshape(C, SEND, C).astype(BF16)


def gate_kernel(x_ref, norms_ref, w_ref, out_ref):
    for a in range(A):
        x = x_ref[a].astype(F32)
        normed = layer_norm(x, norms_ref[0:1], norms_ref[1:2]).astype(BF16)
        out_ref[a] = sigmoid(dot(normed, w_ref[...], ((1,), (0,))))


def product_kernel(in_ref, out_ref, wide, left, right, prod, back):
    wide[...] = in_ref[...].astype(F32).reshape(C * SEND, C)
    for side, matrix in enumerate((left, right)):
        for a in range(A):
            rows = [
                wide[pl.ds((side * A + a) * G + g, C, stride=SEND), :].astype(BF16) for g in range(G)
            ]
            parts = swap_groups(
                [
                    jnp.concatenate([row[r * COLS : (r + 1) * COLS] for row in rows], axis=0)
                    for r in range(ROWS)
                ]
            )
            for b in range(8):
                first = (a * 8 + b) * COLS
                for g in range(G):
                    matrix[first : first + COLS, g * C : (g + 1) * C] = parts[b][
                        g * COLS : (g + 1) * COLS
                    ]
    back[...] = jnp.zeros_like(back)
    for g in range(G):
        prod[g] = dot(right[...], left[:, g * C : (g + 1) * C], ((0,), (0,)))
    for g in range(G):
        for half in range(2):
            firsts = [s // 2 * C + s % 2 * 8 for s in range(half * A, half * A + A)]
            parts = swap_groups(
                [
                    jnp.concatenate(
                        [prod[g, pl.ds(first + b, ROWS, stride=16), :] for first in firsts], axis=0
                    )
                    for b in range(8)
                ]
            )
            for r in range(ROWS):
                for a in range(A):
                    row = (r * COLS + half) * BACK + a * G + g
                    back[pl.ds(row, ROWS, stride=2 * BACK), :] = parts[r][a * ROWS : (a + 1) * ROWS]
    out_ref[...] = back[...].reshape(C, BACK, C).astype(BF16)


def middle_kernel(in_ref, x_ref, gate_ref, norms_ref, w_ref, out_ref, wide, pay):
    wide[...] = in_ref[...].astype(F32).reshape(C * BACK, C)
    pay[...] = jnp.zeros_like(pay)
    gain = jnp.broadcast_to(norms_ref[2:3], (C, C)).T[:, :1]
    bias = jnp.broadcast_to(norms_ref[3:4], (C, C)).T[:, :1]
    for a in range(A):
        prod = jnp.concatenate(
            [wide[pl.ds(a * G + g, C, stride=BACK), :] for g in range(G)], axis=1
        )
        normed = layer_norm(prod, gain, bias, 0).astype(BF16)
        update = dot(normed, w_ref[:C], ((0,), (0,)))
        mid = (x_ref[a].astype(F32) + gate_ref[a] * update).astype(BF16)
        for g in range(G):
            for b in range(8):
                r, t = divmod(8 * a + b, T)
                out_ref[r, t * RI + 16 * g : t * RI + 16 * g + 16, :] = mid[
                    (g * 8 + b) * 16 : (g * 8 + b + 1) * 16
                ]
        att = layer_norm(mid.astype(F32), norms_ref[4:5], norms_ref[5:6]).astype(BF16)
        rows = dot(w_ref[C:], att, ((1,), (1,)))
        for g in range(G):
            first = (a * G + g) * H
            pay[first : first + H, :] = rows[:H, g * C : (g + 1) * C]
    for r in range(ROWS):
        out_ref[r, TURN:, :] = pay[...].astype(BF16)


def qkvg_kernel(in_ref, norms_ref, wqg_ref, wv_ref, wk_ref, q_ref, k_ref, v_ref, g_ref):
    for t in range(T):
        mid = jnp.concatenate([in_ref[r, t * RI : (t + 1) * RI, :] for r in range(ROWS)], axis=0)
        att = layer_norm(mid.astype(F32), norms_ref[4:5], norms_ref[5:6]).astype(BF16)
        keyed = jnp.concatenate(
            [att[r * RI + 16 * g : r * RI + 16 * g + 16] for g in range(G) for r in range(ROWS)], axis=0
        )
        qg = dot(att, wqg_ref[...], ((1,), (0,)))
        q_ref[t] = (qg[:, :C] * DH ** (-0.5)).astype(BF16)
        g_ref[t] = sigmoid(qg[:, C:])
        vals = dot(keyed, wv_ref[...], ((1,), (0,))).astype(BF16)
        v_ref[t] = jnp.concatenate([vals, jnp.ones((N, C), BF16)], axis=1)
        k_ref[t] = dot(wk_ref[...], keyed, ((1,), (1,))).astype(BF16)


def merge_kernel(in_ref, out_ref, parts, rows):
    for b, part in enumerate(swap_groups([in_ref[r, TURN:, :].astype(F32) for r in range(ROWS)])):
        parts[b] = part
    for b in range(8):
        for g in range(G):
            for h in range(H):
                rows[g, pl.ds(h * CJ + b, A, stride=8), :] = parts[b, pl.ds(g * H + h, A, stride=G * H), :]
    out_ref[...] = jnp.concatenate([rows[g] for g in range(G)], axis=1).astype(BF16)


def attend_kernel(
    steps, me_ref, inter_ref, q_ref, k_ref, v_ref, g_ref, mid_ref, cross_ref, key_ref, valid_ref, valid_t_ref, wo_ref,
    *refs,
):
    parts, (out_ref, extra, score_a, score_b, power_a, power_b) = refs[:-6], refs[-6:]
    score, power = (score_a, score_b), (power_a, power_b)
    me = me_ref[0]
    chips = [(me // 2) ^ step for step in steps]
    count = len(chips)
    chunk = count * RI
    late = count == 2
    for n in range(count):
        for other in range(2):
            core = (me % 2) ^ other
            first = chips[n] * RI + core * CJ
            half = parts[other * len(parts) // 2 : (other + 1) * len(parts) // 2]
            part = half[n] if len(half) == count else half[n // 2].at[n % 2]
            for s in range(CJ // 8):
                to = pl.multiple_of(n * RI + core * CJ + 8 * s, 8)
                crossing = cross_ref[pl.ds((first + 8 * s) // MB, 1), :]
                for h in range(H):
                    extra[h, pl.ds(to, 8), :] = (
                        part[h * CJ + 8 * s : h * CJ + 8 * s + 8, :].astype(F32)
                        + inter_ref[h] * crossing
                        + key_ref[...]
                    )
    lane_head = lax.broadcasted_iota(jnp.int32, (chunk, C), 1) // DH

    def rows_of(take):
        return jnp.concatenate([take(pl.ds(pl.multiple_of(chip * RI, RI), RI)) for chip in chips], axis=0)

    valid = rows_of(lambda rows: valid_ref[rows, :])

    def one_column(t, carry):
        queries = rows_of(lambda rows: q_ref[t, rows, :])

        def set_score(h):
            own = jnp.where(lane_head == h, queries, jnp.zeros_like(queries))
            score[h % 2][...] = dot(own, k_ref[t], ((1,), (0,))) + extra[h]

        def weigh(h, total):
            sums = dot(power[h % 2][...], v_ref[t], ((1,), (0,)))
            return jnp.where(lane_head == h, sums[:, :C] / sums[:, C:], total)

        total = jnp.zeros((chunk, C), F32)
        set_score(0)
        for h in range(H + late):
            if h + 1 < H:
                set_score(h + 1)
            if late and h > 0:
                total = weigh(h - 1, total)
            if h < H:
                now = score[h % 2][...]
                highest = jnp.max(now, axis=1, keepdims=True)
                power[h % 2][...] = jnp.exp(now - highest).astype(BF16)
            if not late:
                total = weigh(h, total)
        gated = (rows_of(lambda rows: g_ref[t, rows, :]) * total).astype(BF16)
        update = dot(gated, wo_ref[...], ((1,), (0,)))
        own = pl.ds(pl.multiple_of(t * RI, RI), RI)
        mid = jnp.concatenate([mid_ref[chip, own, :] for chip in chips], axis=0).astype(F32)
        out = (mid + valid * valid_t_ref[t] * update).astype(BF16)
        for n in range(count):
            out_ref[n * T + t] = out[n * RI : (n + 1) * RI]
        return carry

    lax.fori_loop(0, T, one_column, 0)


def order_kernel(me_ref, *refs):
    out_ref = refs[-1]
    for call_at, n, step in [(c, n, step) for c, steps in enumerate(CALLS) for n, step in enumerate(steps)]:
        chip = (me_ref[0] // 2) ^ step
        for t in range(T):
            out_ref[chip * T + t] = refs[call_at][n * T + t]


def on_device(
    pair,
    block_chain,
    block_valid,
    tri_norm_gain,
    tri_norm_bias,
    tri_in_weight,
    tri_gate_weight,
    out_norm_gain,
    out_norm_bias,
    tri_out_weight,
    att_norm_gain,
    att_norm_bias,
    qkvg_weight,
    bias_weight,
    inter_chain,
    att_out_weight,
):
    row_at, col_at = lax.axis_index("row"), lax.axis_index("col")
    both = ("row", "col")
    residue_valid = jnp.repeat(block_valid, MB).astype(F32)
    norms = jnp.stack(
        [tri_norm_gain, tri_norm_bias, out_norm_gain, out_norm_bias, att_norm_gain, att_norm_bias]
    )

    parcels, x = call(
        project_kernel,
        [struct((C, SEND, C)), struct((A, N, C))],
        [
            pltpu.VMEM((RI, CJ, C), BF16),
            pltpu.SMEM((N // MB,), jnp.int32),
            pltpu.VMEM((C,), F32),
            pltpu.VMEM((C,), F32),
            pltpu.VMEM((C, 4 * C), BF16),
            pltpu.VMEM((RI * CJ, C), F32),
            pltpu.VMEM((C * SEND, C), F32),
            pltpu.SemaphoreType.DMA((5,)),
        ],
        [pl.BlockSpec(memory_space=pl.ANY)] * 5,
        mib=60,
    )(pair, block_valid, tri_norm_gain, tri_norm_bias, tri_in_weight)
    gate = call(gate_kernel, struct((A, N, C), F32), [], [VMEM] * 3)(x, norms, tri_gate_weight)
    channel = lax.all_to_all(parcels, both, 0, 0, tiled=True)
    product = call(
        product_kernel,
        struct((C, BACK, C)),
        [
            pltpu.VMEM((C * SEND, C), F32),
            pltpu.VMEM((N, N), BF16),
            pltpu.VMEM((N, N), BF16),
            pltpu.VMEM((G, N, C), F32),
            pltpu.VMEM((C * BACK, C), F32),
        ],
        [VMEM],
    )(channel)
    returned = lax.all_to_all(product, both, 0, 0, tiled=True)

    w_mid = jnp.concatenate([tri_out_weight, jnp.pad(bias_weight.T, ((0, 8 - H), (0, 0)))])
    turned = call(
        middle_kernel,
        struct((ROWS, TURN + PAY, C)),
        [pltpu.VMEM((C * BACK, C), F32), pltpu.VMEM((PAY, C), F32)],
        [VMEM] * 5,
    )(returned, x, gate, norms, w_mid)
    mid = lax.all_to_all(turned, "row", 0, 0, tiled=True)

    valid_t = lax.dynamic_slice_in_dim(residue_valid, (col_at * ROWS + row_at) * T, T)
    valid_rows = jnp.broadcast_to(residue_valid[:, None], (N, C))

    def keyed(values):
        return values.reshape(ROWS, G, 16).transpose(1, 0, 2).reshape(N)

    cross = (block_chain[:, None] != keyed(jnp.repeat(block_chain, MB))[None, :]).astype(F32)
    key_mask = (MASK_NEG * (keyed(residue_valid) - 1.0))[None, :]

    def swap(values, row_xor, col_xor):
        pairs = [
            (r * COLS + c, (r ^ row_xor) * COLS + (c ^ col_xor))
            for r in range(ROWS)
            for c in range(COLS)
        ]
        return lax.ppermute(values, both, pairs)

    merged = call(
        merge_kernel,
        struct((H * CJ, N)),
        [pltpu.VMEM((ROWS, PAY, C), F32), pltpu.VMEM((G, H * CJ, C), F32)],
        [VMEM],
    )(mid)
    hold = lax.optimization_barrier

    def core(values):
        return swap(values, 0, 1)

    one, merged2 = swap(merged, 0, 4), core(merged)
    wqg = jnp.concatenate([qkvg_weight[:, :C], qkvg_weight[:, 3 * C :]], axis=1)
    q, k, v, g = call(
        qkvg_kernel,
        [struct((T, N, C)), struct((T, C, N)), struct((T, N, 2 * C)), struct((T, N, C), F32)],
        [],
        [VMEM] * 5,
    )(mid, norms, wqg, qkvg_weight[:, 2 * C : 3 * C], qkvg_weight[:, C : 2 * C].T)

    merged, q, k, v, g = hold((merged, q, k, v, g))
    two, three, beside = [swap(merged, 0, step) for step in (8, 12, 2)]

    def attend(steps, *parts):
        chunk = len(steps) * RI
        return call(
            functools.partial(attend_kernel, steps),
            struct((len(steps) * T, RI, C)),
            [pltpu.VMEM((H, chunk, N), F32)]
            + [pltpu.VMEM((chunk, N), F32)] * 2
            + [pltpu.VMEM((chunk, N), BF16)] * 2,
            [SMEM, SMEM] + [VMEM] * 8 + [SMEM, VMEM] + [VMEM] * len(parts),
            pl.CostEstimate(flops=1 << 20, bytes_accessed=1 << 16, transcendentals=0),
        )(
            col_at[None], inter_chain, q, k, v, g, mid, cross, key_mask, valid_rows, valid_t, att_out_weight,
            *parts,
        )

    one_across = swap(one, ROWS // 2, 2)
    near = hold((merged, one, merged2, core(one)))
    outs = [attend(CALLS[0], *near)]
    outs[0], two, three, beside, one_across = hold((outs[0], two, three, beside, one_across))
    column, across = jnp.stack([two, three]), jnp.stack([beside, one_across])
    far = swap(column, ROWS // 2, 2)
    column, across, column2, across2 = hold((column, across, core(column), core(across)))
    outs.append(attend(CALLS[1], column, across, column2, across2))
    outs[1], far = hold((outs[1], far))
    outs.append(attend(CALLS[2], far, core(far)))
    out = call(order_kernel, struct((CJ, RI, C)), [], [SMEM] + [VMEM] * 3)(col_at[None], *outs)
    home = lax.all_to_all(out, "row", 0, 0, tiled=True)
    return call(turn_back_kernel, struct((RI, CJ, C)), [pltpu.VMEM((RI * CJ, C), F32)], [VMEM])(home)


def solution(mesh):
    placed = (P("row", "col", None),) + (P(),) * 15
    return jax.shard_map(
        on_device, mesh=mesh, in_specs=placed, out_specs=P("row", "col", None), check_vma=False
    )
```

```python
import functools

import jax
import jax.numpy as jnp
from jax import lax
from jax.experimental import pallas as pl
from jax.experimental.pallas import tpu as pltpu
from jax.sharding import PartitionSpec as P

H = 4
DH = 32
MB = 64
C = 128
N = 640
ROWS = 8
COLS = 16
RI = N // ROWS
CJ = N // COLS
T = CJ // ROWS
SEND = 56
BACK = 32
G = RI // 16
A = CJ // 8
TURN = T * RI
PAY = 112
CALLS = ((0, 2), (4, 6, 1, 3), (5, 7))

MASK_NEG = 10000.0
EPS = 1e-05

F32 = jnp.float32
BF16 = jnp.bfloat16
VMEM = pl.BlockSpec(memory_space=pltpu.VMEM)
SMEM = pl.BlockSpec(memory_space=pltpu.SMEM)


def dot(a, b, over):
    return lax.dot_general(a, b, (over, ((), ())), preferred_element_type=F32)


def layer_norm(values, gain, shift, axis=-1):
    middle = jnp.mean(values, axis=axis, keepdims=True)
    centred = values - middle
    spread = jnp.mean(centred * centred, axis=axis, keepdims=True)
    return centred * lax.rsqrt(spread + EPS) * gain + shift


def sigmoid(x):
    return 0.5 * jnp.tanh(0.5 * x) + 0.5


def call(kernel, out_shape, scratch, specs, cost=None, mib=24):
    return pl.pallas_call(
        kernel,
        out_shape=out_shape,
        in_specs=specs,
        out_specs=jax.tree.map(lambda _: VMEM, out_shape),
        scratch_shapes=scratch,
        compiler_params=pltpu.CompilerParams(vmem_limit_bytes=mib * 1024 * 1024),
        cost_estimate=cost,
    )


def struct(shape, dtype=BF16):
    return jax.ShapeDtypeStruct(shape, dtype)


def swap_groups(arrays):
    arrays = list(arrays)
    group = lax.broadcasted_iota(jnp.int32, arrays[0].shape, 1) // 16
    for bit in (1, 2, 4):
        high = (group & bit) != 0
        for p in range(8):
            if not p & bit:
                one, two = arrays[p], arrays[p | bit]
                arrays[p] = jnp.where(high, pltpu.roll(two, 16 * bit, 1), one)
                arrays[p | bit] = jnp.where(high, two, pltpu.roll(one, C - 16 * bit, 1))
    return arrays


def turn_back_kernel(in_ref, out_ref, wide):
    for j in range(CJ):
        wide[pl.ds(j, RI, stride=CJ), :] = in_ref[j].astype(F32)
    out_ref[...] = wide[...].reshape(RI, CJ, C).astype(BF16)


def project_kernel(
    pair_hbm, valid_hbm, gain_hbm, bias_hbm, w_hbm, out_ref, x_ref,
    pair_ref, valid_ref, gain_ref, bias_ref, w_ref, pairs, wide, sems,
):
    copies = [
        pltpu.make_async_copy(source, target, sems.at[n])
        for n, (source, target) in enumerate(
            (
                (pair_hbm, pair_ref),
                (valid_hbm, valid_ref),
                (gain_hbm, gain_ref),
                (bias_hbm, bias_ref),
                (w_hbm, w_ref),
            )
        )
    ]
    for copy in copies:
        copy.start()
    wide[...] = jnp.zeros_like(wide)
    for copy in copies:
        copy.wait()
    pairs[...] = pair_ref[...].astype(F32).reshape(RI * CJ, C)
    weight = w_ref[...].T
    for a in range(A):
        x = jnp.concatenate(
            [
                pairs[pl.ds(16 * g * CJ + 8 * a + b, 16, stride=CJ), :]
                for g in range(G)
                for b in range(8)
            ],
            axis=0,
        )
        x_ref[a] = x.astype(BF16)
        normed = layer_norm(x, gain_ref[...][None, :], bias_ref[...][None, :]).astype(BF16)
        proj = dot(weight, normed, ((1,), (1,)))
        valid_j = valid_ref[(lax.axis_index("col") * A + a) // (MB // 8)]
        for g in range(G):
            lanes = slice(g * C, (g + 1) * C)
            mask = (valid_ref[(lax.axis_index("row") * G + g) // (MB // 16)] * valid_j).astype(F32)
            for side in range(2):
                gate = proj[2 * side * C : (2 * side + 1) * C, lanes]
                value = proj[(2 * side + 1) * C : (2 * side + 2) * C, lanes]
                wide[pl.ds((side * A + a) * G + g, C, stride=SEND), :] = mask * sigmoid(gate) * value
    out_ref[...] = wide[...].reshape(C, SEND, C).astype(BF16)


def gate_kernel(x_ref, norms_ref, w_ref, out_ref):
    for a in range(A):
        x = x_ref[a].astype(F32)
        normed = layer_norm(x, norms_ref[0:1], norms_ref[1:2]).astype(BF16)
        out_ref[a] = sigmoid(dot(normed, w_ref[...], ((1,), (0,))))


def product_kernel(in_ref, out_ref, wide, left, right, prod, back):
    wide[...] = in_ref[...].astype(F32).reshape(C * SEND, C)
    for side, matrix in enumerate((left, right)):
        for a in range(A):
            rows = [
                wide[pl.ds((side * A + a) * G + g, C, stride=SEND), :].astype(BF16) for g in range(G)
            ]
            parts = swap_groups(
                [
                    jnp.concatenate([row[r * COLS : (r + 1) * COLS] for row in rows], axis=0)
                    for r in range(ROWS)
                ]
            )
            for b in range(8):
                first = (a * 8 + b) * COLS
                for g in range(G):
                    matrix[first : first + COLS, g * C : (g + 1) * C] = parts[b][
                        g * COLS : (g + 1) * COLS
                    ]
    back[...] = jnp.zeros_like(back)
    for g in range(G):
        prod[g] = dot(right[...], left[:, g * C : (g + 1) * C], ((0,), (0,)))
    for g in range(G):
        for half in range(2):
            firsts = [s // 2 * C + s % 2 * 8 for s in range(half * A, half * A + A)]
            parts = swap_groups(
                [
                    jnp.concatenate(
                        [prod[g, pl.ds(first + b, ROWS, stride=16), :] for first in firsts], axis=0
                    )
                    for b in range(8)
                ]
            )
            for r in range(ROWS):
                for a in range(A):
                    row = (r * COLS + half) * BACK + a * G + g
                    back[pl.ds(row, ROWS, stride=2 * BACK), :] = parts[r][a * ROWS : (a + 1) * ROWS]
    out_ref[...] = back[...].reshape(C, BACK, C).astype(BF16)


def middle_kernel(in_ref, x_ref, gate_ref, norms_ref, w_ref, out_ref, wide, pay):
    wide[...] = in_ref[...].astype(F32).reshape(C * BACK, C)
    pay[...] = jnp.zeros_like(pay)
    gain = jnp.broadcast_to(norms_ref[2:3], (C, C)).T[:, :1]
    bias = jnp.broadcast_to(norms_ref[3:4], (C, C)).T[:, :1]
    for a in range(A):
        prod = jnp.concatenate(
            [wide[pl.ds(a * G + g, C, stride=BACK), :] for g in range(G)], axis=1
        )
        normed = layer_norm(prod, gain, bias, 0).astype(BF16)
        update = dot(normed, w_ref[:C], ((0,), (0,)))
        mid = (x_ref[a].astype(F32) + gate_ref[a] * update).astype(BF16)
        for g in range(G):
            for b in range(8):
                r, t = divmod(8 * a + b, T)
                out_ref[r, t * RI + 16 * g : t * RI + 16 * g + 16, :] = mid[
                    (g * 8 + b) * 16 : (g * 8 + b + 1) * 16
                ]
        att = layer_norm(mid.astype(F32), norms_ref[4:5], norms_ref[5:6]).astype(BF16)
        rows = dot(w_ref[C:], att, ((1,), (1,)))
        for g in range(G):
            first = (a * G + g) * H
            pay[first : first + H, :] = rows[:H, g * C : (g + 1) * C]
    for r in range(ROWS):
        out_ref[r, TURN:, :] = pay[...].astype(BF16)


def qkvg_kernel(in_ref, norms_ref, wqg_ref, wv_ref, wk_ref, q_ref, k_ref, v_ref, g_ref):
    for t in range(T):
        mid = jnp.concatenate([in_ref[r, t * RI : (t + 1) * RI, :] for r in range(ROWS)], axis=0)
        att = layer_norm(mid.astype(F32), norms_ref[4:5], norms_ref[5:6]).astype(BF16)
        keyed = jnp.concatenate(
            [att[r * RI + 16 * g : r * RI + 16 * g + 16] for g in range(G) for r in range(ROWS)], axis=0
        )
        qg = dot(att, wqg_ref[...], ((1,), (0,)))
        q_ref[t] = (qg[:, :C] * DH ** (-0.5)).astype(BF16)
        g_ref[t] = sigmoid(qg[:, C:])
        vals = dot(keyed, wv_ref[...], ((1,), (0,))).astype(BF16)
        v_ref[t] = jnp.concatenate([vals, jnp.ones((N, C), BF16)], axis=1)
        k_ref[t] = dot(wk_ref[...], keyed, ((1,), (1,))).astype(BF16)


def merge_kernel(in_ref, out_ref, parts, rows):
    for b, part in enumerate(swap_groups([in_ref[r, TURN:, :].astype(F32) for r in range(ROWS)])):
        parts[b] = part
    for b in range(8):
        for g in range(G):
            for h in range(H):
                rows[g, pl.ds(h * CJ + b, A, stride=8), :] = parts[b, pl.ds(g * H + h, A, stride=G * H), :]
    out_ref[...] = jnp.concatenate([rows[g] for g in range(G)], axis=1).astype(BF16)


def attend_kernel(
    steps, me_ref, inter_ref, q_ref, k_ref, v_ref, g_ref, mid_ref, cross_ref, key_ref, valid_ref, valid_t_ref, wo_ref,
    *refs,
):
    parts, (out_ref, extra, score_a, score_b, power_a, power_b) = refs[:-6], refs[-6:]
    score, power = (score_a, score_b), (power_a, power_b)
    me = me_ref[0]
    chips = [(me // 2) ^ step for step in steps]
    count = len(chips)
    chunk = count * RI
    late = count == 2
    for n in range(count):
        for other in range(2):
            core = (me % 2) ^ other
            first = chips[n] * RI + core * CJ
            half = parts[other * len(parts) // 2 : (other + 1) * len(parts) // 2]
            part = half[n] if len(half) == count else half[n // 2].at[n % 2]
            for s in range(CJ // 8):
                to = pl.multiple_of(n * RI + core * CJ + 8 * s, 8)
                crossing = cross_ref[pl.ds((first + 8 * s) // MB, 1), :]
                for h in range(H):
                    extra[h, pl.ds(to, 8), :] = (
                        part[h * CJ + 8 * s : h * CJ + 8 * s + 8, :].astype(F32)
                        + inter_ref[h] * crossing
                        + key_ref[...]
                    )
    lane_head = lax.broadcasted_iota(jnp.int32, (chunk, C), 1) // DH

    def rows_of(take):
        return jnp.concatenate([take(pl.ds(pl.multiple_of(chip * RI, RI), RI)) for chip in chips], axis=0)

    valid = rows_of(lambda rows: valid_ref[rows, :])

    def one_column(t, carry):
        queries = rows_of(lambda rows: q_ref[t, rows, :])

        def set_score(h):
            own = jnp.where(lane_head == h, queries, jnp.zeros_like(queries))
            score[h % 2][...] = dot(own, k_ref[t], ((1,), (0,))) + extra[h]

        def weigh(h, total):
            sums = dot(power[h % 2][...], v_ref[t], ((1,), (0,)))
            return jnp.where(lane_head == h, sums[:, :C] / sums[:, C:], total)

        total = jnp.zeros((chunk, C), F32)
        set_score(0)
        for h in range(H + late):
            if h + 1 < H:
                set_score(h + 1)
            if late and h > 0:
                total = weigh(h - 1, total)
            if h < H:
                now = score[h % 2][...]
                highest = jnp.max(now, axis=1, keepdims=True)
                power[h % 2][...] = jnp.exp(now - highest).astype(BF16)
            if not late:
                total = weigh(h, total)
        gated = (rows_of(lambda rows: g_ref[t, rows, :]) * total).astype(BF16)
        update = dot(gated, wo_ref[...], ((1,), (0,)))
        own = pl.ds(pl.multiple_of(t * RI, RI), RI)
        mid = jnp.concatenate([mid_ref[chip, own, :] for chip in chips], axis=0).astype(F32)
        out = (mid + valid * valid_t_ref[t] * update).astype(BF16)
        for n in range(count):
            out_ref[n * T + t] = out[n * RI : (n + 1) * RI]
        return carry

    lax.fori_loop(0, T, one_column, 0)


def order_kernel(me_ref, *refs):
    out_ref = refs[-1]
    for call_at, n, step in [(c, n, step) for c, steps in enumerate(CALLS) for n, step in enumerate(steps)]:
        chip = (me_ref[0] // 2) ^ step
        for t in range(T):
            out_ref[chip * T + t] = refs[call_at][n * T + t]


def on_device(
    pair,
    block_chain,
    block_valid,
    tri_norm_gain,
    tri_norm_bias,
    tri_in_weight,
    tri_gate_weight,
    out_norm_gain,
    out_norm_bias,
    tri_out_weight,
    att_norm_gain,
    att_norm_bias,
    qkvg_weight,
    bias_weight,
    inter_chain,
    att_out_weight,
):
    row_at, col_at = lax.axis_index("row"), lax.axis_index("col")
    both = ("row", "col")
    residue_valid = jnp.repeat(block_valid, MB).astype(F32)
    norms = jnp.stack(
        [tri_norm_gain, tri_norm_bias, out_norm_gain, out_norm_bias, att_norm_gain, att_norm_bias]
    )

    parcels, x = call(
        project_kernel,
        [struct((C, SEND, C)), struct((A, N, C))],
        [
            pltpu.VMEM((RI, CJ, C), BF16),
            pltpu.SMEM((N // MB,), jnp.int32),
            pltpu.VMEM((C,), F32),
            pltpu.VMEM((C,), F32),
            pltpu.VMEM((C, 4 * C), BF16),
            pltpu.VMEM((RI * CJ, C), F32),
            pltpu.VMEM((C * SEND, C), F32),
            pltpu.SemaphoreType.DMA((5,)),
        ],
        [pl.BlockSpec(memory_space=pl.ANY)] * 5,
        mib=60,
    )(pair, block_valid, tri_norm_gain, tri_norm_bias, tri_in_weight)
    gate = call(gate_kernel, struct((A, N, C), F32), [], [VMEM] * 3)(x, norms, tri_gate_weight)
    channel = lax.all_to_all(parcels, both, 0, 0, tiled=True)
    product = call(
        product_kernel,
        struct((C, BACK, C)),
        [
            pltpu.VMEM((C * SEND, C), F32),
            pltpu.VMEM((N, N), BF16),
            pltpu.VMEM((N, N), BF16),
            pltpu.VMEM((G, N, C), F32),
            pltpu.VMEM((C * BACK, C), F32),
        ],
        [VMEM],
    )(channel)
    returned = lax.all_to_all(product, both, 0, 0, tiled=True)

    w_mid = jnp.concatenate([tri_out_weight, jnp.pad(bias_weight.T, ((0, 8 - H), (0, 0)))])
    turned = call(
        middle_kernel,
        struct((ROWS, TURN + PAY, C)),
        [pltpu.VMEM((C * BACK, C), F32), pltpu.VMEM((PAY, C), F32)],
        [VMEM] * 5,
    )(returned, x, gate, norms, w_mid)
    mid = lax.all_to_all(turned, "row", 0, 0, tiled=True)

    valid_t = lax.dynamic_slice_in_dim(residue_valid, (col_at * ROWS + row_at) * T, T)
    valid_rows = jnp.broadcast_to(residue_valid[:, None], (N, C))

    def keyed(values):
        return values.reshape(ROWS, G, 16).transpose(1, 0, 2).reshape(N)

    cross = (block_chain[:, None] != keyed(jnp.repeat(block_chain, MB))[None, :]).astype(F32)
    key_mask = (MASK_NEG * (keyed(residue_valid) - 1.0))[None, :]

    def swap(values, row_xor, col_xor):
        pairs = [
            (r * COLS + c, (r ^ row_xor) * COLS + (c ^ col_xor))
            for r in range(ROWS)
            for c in range(COLS)
        ]
        return lax.ppermute(values, both, pairs)

    merged = call(
        merge_kernel,
        struct((H * CJ, N)),
        [pltpu.VMEM((ROWS, PAY, C), F32), pltpu.VMEM((G, H * CJ, C), F32)],
        [VMEM],
    )(mid)
    hold = lax.optimization_barrier

    def core(values):
        return swap(values, 0, 1)

    one, merged2 = swap(merged, 0, 4), core(merged)
    wqg = jnp.concatenate([qkvg_weight[:, :C], qkvg_weight[:, 3 * C :]], axis=1)
    q, k, v, g = call(
        qkvg_kernel,
        [struct((T, N, C)), struct((T, C, N)), struct((T, N, 2 * C)), struct((T, N, C), F32)],
        [],
        [VMEM] * 5,
    )(mid, norms, wqg, qkvg_weight[:, 2 * C : 3 * C], qkvg_weight[:, C : 2 * C].T)

    merged, q, k, v, g = hold((merged, q, k, v, g))
    two, three, beside = [swap(merged, 0, step) for step in (8, 12, 2)]

    def attend(steps, *parts):
        chunk = len(steps) * RI
        return call(
            functools.partial(attend_kernel, steps),
            struct((len(steps) * T, RI, C)),
            [pltpu.VMEM((H, chunk, N), F32)]
            + [pltpu.VMEM((chunk, N), F32)] * 2
            + [pltpu.VMEM((chunk, N), BF16)] * 2,
            [SMEM, SMEM] + [VMEM] * 8 + [SMEM, VMEM] + [VMEM] * len(parts),
            pl.CostEstimate(flops=1 << 20, bytes_accessed=1 << 16, transcendentals=0),
        )(
            col_at[None], inter_chain, q, k, v, g, mid, cross, key_mask, valid_rows, valid_t, att_out_weight,
            *parts,
        )

    one_across = swap(merged, ROWS // 2, 6)
    near = hold((merged, one, merged2, core(one)))
    outs = [attend(CALLS[0], *near)]
    outs[0], two, three, beside, one_across = hold((outs[0], two, three, beside, one_across))
    column, across = jnp.stack([two, three]), jnp.stack([beside, one_across])
    far = swap(column, ROWS // 2, 2)
    column, across, column2, across2 = hold((column, across, core(column), core(across)))
    outs.append(attend(CALLS[1], column, across, column2, across2))
    outs[1], far = hold((outs[1], far))
    outs.append(attend(CALLS[2], far, core(far)))
    out = call(order_kernel, struct((CJ, RI, C)), [], [SMEM] + [VMEM] * 3)(col_at[None], *outs)
    home = lax.all_to_all(out, "row", 0, 0, tiled=True)
    return call(turn_back_kernel, struct((RI, CJ, C)), [pltpu.VMEM((RI * CJ, C), F32)], [VMEM])(home)


def solution(mesh):
    placed = (P("row", "col", None),) + (P(),) * 15
    return jax.shard_map(
        on_device, mesh=mesh, in_specs=placed, out_specs=P("row", "col", None), check_vma=False
    )
```
